32 devices in a mesh: groups: 2 (over y), segment: 8 (over z, x), template: 2 (over core).
Axes of the slice: x: 2, y: 2, z: 4, core: 2. Of those that a mesh axis runs over, the one named last changes fastest.
Arguments:
- strain_frames: bfloat16 [64, 16384], P('segment'), may hold values from -6 to 6
- frame_slot: int32 [8, 8], replicated, may hold values from 0 to 7, as said below
- templates: bfloat16 [4, 2, 131072], P(('groups', 'template'), None, 'segment'), parts along dimension 0, may hold values from -6 to 6
- bin_edges: int32 [4, 3], P(('groups', 'template')), parts along dimension 0, may hold values from 16384 to 114687, as said below
Outputs:
- snr_series: bfloat16 [8, 4, 131072], P('segment', ('groups', 'template')), parts along dimension 1
- chisq_series: bfloat16 [8, 4, 131072], P('segment', ('groups', 'template')), parts along dimension 1
- peak_newsnr: float32 [8, 4], P('segment', ('groups', 'template')), parts along dimension 1
The draws below stay inside these ranges and needn't reach their ends.
There are 2 independent parts, one for each index of `groups`. The reference program is written for one: setup_inputs(seed, part) draws one part's arguments, and reference() takes and returns one part's arrays. A program takes and returns all parts, laid end to end along the dimension named above; an argument that names none is the same for every part. Nothing has to cross between parts.
Inputs may be any that keep to these rules, and one draw needn't show every extreme that they name: Each column frame_slot[:, j] is a permutation of 0 to 7. `bin_edges`: edge number e of a template lies in [(2 e + 1) * 16384, (2 e + 3) * 16384), so the edges rise.
All inputs are finite; a program needn't handle non-finite values.
Results may differ from the reference program's by a relative error of at most 0.011.
Values may be sent and summed in bfloat16 or wider, within the bound.
A program may use at most 64 MiB of HBM per device.

```python
import math
import jax
import jax.numpy as jnp
from jax import lax

RADIX_A = 64
RADIX_B = 32
RADIX_C = 128
KB = 131072
NSEG = 8
FRAMELEN = 16384
FRAMES = 64
TEMPLATES = 2


def shuffle_column(single_key):
    return jax.random.permutation(single_key, NSEG)


def draw_frame_slot(key, part):
    column_keys = jax.random.split(key, NSEG)
    columns = jax.vmap(shuffle_column)(column_keys)
    return jnp.transpose(columns).astype(jnp.int32)


def draw_bin_edges(key, part):
    offsets = jax.random.randint(key, (TEMPLATES, 3), 0, KB // 4)
    offsets = offsets.at[0, 0].set(0)
    offsets = offsets.at[TEMPLATES - 1, 2].set(KB // 4 - 1)
    bases = KB // 8 * jnp.array([1, 3, 5], dtype=jnp.int32)
    return (offsets + bases[None, :]).astype(jnp.int32)


def shard_levels(stream_key, shape, cuts, smallest, largest):
    def one(dim, shards_of):
        steps = jax.random.uniform(jax.random.fold_in(jax.random.fold_in(stream_key, 6), dim), (shards_of,), jnp.float32, smallest / len(cuts), largest / len(cuts))
        return jnp.repeat(jnp.exp(steps), shape[dim] // shards_of).reshape((-1,) + (1,) * (len(shape) - dim - 1))

    loudness = one(*cuts[0])
    for cut in cuts[1:]:
        loudness = loudness * one(*cut)
    return loudness


def normal_values(own_key, extent, deviation, limit, cuts=(), held_as=jnp.bfloat16):
    loudness = shard_levels(own_key, extent, cuts, -0.22, 0.18) if cuts else 1.0
    values = jax.random.normal(own_key, extent, jnp.float32) * deviation * loudness
    return jnp.minimum(jnp.maximum(values, -limit), limit).astype(held_as)


def setup_inputs(seed: int = 0, part: int = 0) -> dict:
    keys = jax.random.split(jax.random.key(seed), 5)
    part_splits = jax.random.split(jax.random.fold_in(keys[4], part), 5)
    return {
        "strain_frames": normal_values(keys[0], (FRAMES, FRAMELEN), 1.0, 6.0, ((0, 8),)),
        "frame_slot": draw_frame_slot(jax.random.fold_in(keys[4], 71), part),
        "templates": normal_values(part_splits[2], (TEMPLATES, 2, KB), 1.0, 6.0, ((0, 2), (2, 8))),
        "bin_edges": draw_bin_edges(jax.random.fold_in(jax.random.fold_in(keys[4], part), 71), part),
    }


def dft_table(length, orient):
    counter = jnp.arange(length, dtype=jnp.int32)
    product = counter[:, None] * counter[None, :] % length
    angles = orient * 2.0 * math.pi / length * product.astype(jnp.float32)
    cosine = jnp.cos(angles)
    sine = jnp.sin(angles)
    upper = jnp.stack([cosine, -sine], axis=1)
    lower = jnp.stack([sine, cosine], axis=1)
    return jnp.stack([upper, lower], axis=0).astype(jnp.bfloat16)

def rotate(values, phase_index, modulus, orient):
    angles = orient * 2.0 * math.pi / modulus * (phase_index % modulus).astype(jnp.float32)
    cosine = jnp.cos(angles)
    sine = jnp.sin(angles)
    real_part = values[0] * cosine - values[1] * sine
    imag_part = values[0] * sine + values[1] * cosine
    return jnp.stack([real_part, imag_part]).astype(jnp.bfloat16)

def product_level(form, table, values):
    return jnp.einsum(form, table.astype(jnp.float32), values.astype(jnp.float32), precision=lax.Precision.HIGHEST)

def transform(signal, orient):
    length = RADIX_A * RADIX_B * RADIX_C
    inner = RADIX_B * RADIX_C
    start = signal.reshape(2, RADIX_A, inner)
    level_one = product_level('ckdp,dpq->ckq', dft_table(RADIX_A, orient), start)
    grid_one = jnp.arange(RADIX_A, dtype=jnp.int32)[:, None] * jnp.arange(inner, dtype=jnp.int32)[None, :]
    turned = rotate(level_one, grid_one, length, orient).reshape(2, RADIX_A, RADIX_B, RADIX_C)
    level_two = product_level('cjdp,dkpr->ckjr', dft_table(RADIX_B, orient), turned)
    grid_two = jnp.arange(RADIX_B, dtype=jnp.int32)[:, None] * jnp.arange(RADIX_C, dtype=jnp.int32)[None, :]
    turned_two = rotate(level_two, grid_two, inner, orient)
    level_three = product_level('cldr,dkjr->ckjl', dft_table(RADIX_C, orient), turned_two)
    return jnp.transpose(level_three, (0, 3, 2, 1)).reshape(2, length)

def filter_template(spectrum, template, edges):
    length = RADIX_A * RADIX_B * RADIX_C
    kept = length // 2
    temp_real = template[0].astype(jnp.float32)
    temp_imag = template[1].astype(jnp.float32)
    corr_real = spectrum[0] * temp_real + spectrum[1] * temp_imag
    corr_imag = spectrum[1] * temp_real - spectrum[0] * temp_imag
    power = temp_real * temp_real + temp_imag * temp_imag
    total = jnp.sum(power)
    bin_index = jnp.arange(kept, dtype=jnp.int32)
    label = (bin_index >= edges[0]).astype(jnp.int32) + (bin_index >= edges[1]).astype(jnp.int32) + (bin_index >= edges[2]).astype(jnp.int32)
    padding = jnp.zeros((2, length - kept), jnp.bfloat16)
    pieces = []
    shares = []
    for number in range(4):
        inside = (label == number).astype(jnp.float32)
        shares.append(jnp.sum(power * inside) / total)
        masked = jnp.stack([corr_real * inside, corr_imag * inside]).astype(jnp.bfloat16)
        series = transform(jnp.concatenate([masked, padding], axis=1), 1.0) / length
        pieces.append(series[:, length // 4:length // 4 + kept])
    summed = pieces[0] + pieces[1] + pieces[2] + pieces[3]
    scale = length / total
    snr = jnp.sqrt((summed[0] * summed[0] + summed[1] * summed[1]) * scale)
    chisq = jnp.zeros_like(snr)
    for number in range(4):
        diff_real = pieces[number][0] - shares[number] * summed[0]
        diff_imag = pieces[number][1] - shares[number] * summed[1]
        chisq = chisq + diff_real * diff_real + diff_imag * diff_imag
    chisq = chisq * scale
    reduced = chisq / 6.0
    weighted = snr * ((1.0 + reduced * reduced * reduced) / 2.0) ** (-1.0 / 6.0)
    newsnr = jnp.where(reduced > 1.0, weighted, snr)
    return (snr.astype(jnp.bfloat16), chisq.astype(jnp.bfloat16), jnp.max(newsnr))

def reference(strain_frames, frame_slot, templates, bin_edges):
    count = frame_slot.shape[0]
    frame_length = strain_frames.shape[1]
    length = RADIX_A * RADIX_B * RADIX_C
    kept = length // 2
    grouped = strain_frames.reshape(count, count, frame_length)

    def gather_half(half):
        column = lax.dynamic_index_in_dim(frame_slot, half, 1, keepdims=False)
        order = jnp.argsort(column, stable=True).astype(jnp.int32)
        owned = lax.dynamic_index_in_dim(grouped, half, 1, keepdims=False)
        return owned[order].reshape(kept)
    halves = lax.map(gather_half, jnp.arange(count, dtype=jnp.int32))
    padded = jnp.concatenate([halves, jnp.zeros((1, kept), jnp.bfloat16)], axis=0)

    def one_segment(index):
        window = lax.dynamic_slice_in_dim(padded, index, 2, 0).reshape(length)
        signal = jnp.stack([window, jnp.zeros_like(window)])
        spectrum = transform(signal, -1.0)[:, :kept]

        def one_template(number):
            template = lax.dynamic_index_in_dim(templates, number, 0, keepdims=False)
            edges = lax.dynamic_index_in_dim(bin_edges, number, 0, keepdims=False)
            return filter_template(spectrum, template, edges)
        return lax.map(one_template, jnp.arange(templates.shape[0], dtype=jnp.int32))
    snr_series, chisq_series, peak_newsnr = lax.map(one_segment, jnp.arange(count, dtype=jnp.int32))
    return (snr_series, chisq_series, peak_newsnr)
```

```python
import functools
import math

import jax
import jax.numpy as jnp
import numpy as np
from jax import lax
from jax.experimental import pallas as pl
from jax.experimental.pallas import tpu as pltpu
from jax.sharding import PartitionSpec as P

RADIX_A = 64
RADIX_B = 32
RADIX_C = 128
LENGTH = RADIX_A * RADIX_B * RADIX_C
INNER = RADIX_B * RADIX_C
KEPT = LENGTH // 2
SUBROWS = 4
WIDE = INNER // 2
F32 = jnp.float32
BF16 = jnp.bfloat16


def dft_table(length, orient):
    counter = np.arange(length)
    angles = orient * 2.0 * math.pi / length * (counter[:, None] * counter[None, :] % length)
    cosine, sine = np.cos(angles), np.sin(angles)
    upper = np.stack([cosine, -sine], axis=1)
    lower = np.stack([sine, cosine], axis=1)
    return np.stack([upper, lower], axis=0).astype(np.float32)


def tables():
    base = dft_table(RADIX_A, -1.0)[:, :, 0, :]
    first_fwd = np.zeros((SUBROWS, 2, RADIX_A, RADIX_A, SUBROWS), np.float32)
    for sub in range(SUBROWS):
        first_fwd[sub, :, :, :, sub] = base
    first_fwd = first_fwd.reshape(SUBROWS * 2 * RADIX_A, RADIX_A * SUBROWS)
    base = dft_table(RADIX_A, 1.0)[:, :, :, : RADIX_A // 2]
    first_inv = np.zeros((2, 2, RADIX_A, 2, RADIX_A // 2, 2), np.float32)
    for half in range(2):
        first_inv[half, :, :, :, :, half] = base
    first_inv = first_inv.reshape(4 * RADIX_A, 2 * RADIX_A)
    third_fwd = dft_table(RADIX_C, -1.0)[:, : RADIX_C // 2].reshape(RADIX_C, 2 * RADIX_C)
    low = RADIX_C // 4
    third_inv = dft_table(RADIX_C, 1.0)[:, low : low + RADIX_C // 2].reshape(RADIX_C, 2 * RADIX_C)
    third_inv = third_inv.astype(BF16).astype(np.float32) / LENGTH
    k1 = np.arange(RADIX_A)[None, :, None]
    q1 = np.arange(RADIX_B)[:, None, None]
    q2 = np.arange(RADIX_C)[None, None, :]
    angle = 2.0 * math.pi / LENGTH * (k1 * (RADIX_C * q1 + q2) % LENGTH)
    turn_one = np.stack([np.cos(angle), np.sin(angle)]).astype(np.float32)
    angle = 2.0 * math.pi / INNER * (q1 * q2 % INNER)
    turn_two = np.stack([np.cos(angle), np.sin(angle)]).astype(np.float32)
    turn_two = np.broadcast_to(turn_two, (2, RADIX_B, 8, RADIX_C)).copy()
    return (
        first_fwd.astype(BF16),
        first_inv.astype(BF16),
        third_fwd.astype(BF16),
        third_inv.astype(BF16),
        turn_one,
        turn_two,
    )


def cadd(a, b):
    return (a[0] + b[0], a[1] + b[1])


def csub(a, b):
    return (a[0] - b[0], a[1] - b[1])


def quarter(a, orient):
    return (-a[1], a[0]) if orient > 0 else (a[1], -a[0])


def spin(a, eighths, orient):
    eighths = eighths % 32
    if eighths == 0:
        return a
    if eighths == 8:
        return quarter(a, orient)
    if eighths == 4:
        root = math.sqrt(0.5)
        b = quarter(a, orient)
        return ((a[0] + b[0]) * root, (a[1] + b[1]) * root)
    angle = orient * 2.0 * math.pi * eighths / 32
    cosine, sine = math.cos(angle), math.sin(angle)
    return (a[0] * cosine - a[1] * sine, a[0] * sine + a[1] * cosine)


def dft4(x, orient):
    a, b = cadd(x[0], x[2]), csub(x[0], x[2])
    c, d = cadd(x[1], x[3]), quarter(csub(x[1], x[3]), orient)
    return [cadd(a, c), cadd(b, d), csub(a, c), csub(b, d)]


def dft8(x, orient):
    even = dft4(x[0::2], orient)
    odd = dft4(x[1::2], orient)
    odd = [spin(v, 4 * k, orient) for k, v in enumerate(odd)]
    return [cadd(e, o) for e, o in zip(even, odd)] + [csub(e, o) for e, o in zip(even, odd)]


def middle(level_ref, per_row, orient, turn_one_ref, turn_two_ref, turned_ref):
    def turn(value, cosine, sine):
        if orient < 0:
            return (value[0] * cosine + value[1] * sine, value[1] * cosine - value[0] * sine)
        return (value[0] * cosine - value[1] * sine, value[0] * sine + value[1] * cosine)

    def group(g, carry):
        start = pl.multiple_of(g * 8, 8)
        rows = pl.ds(start, 8)

        def load(q1):
            block, lane = q1 // per_row, (q1 % per_row) * RADIX_C
            lanes = slice(lane, lane + RADIX_C)
            real = level_ref[pl.ds(pl.multiple_of(block * 2 * RADIX_A + start, 8), 8), lanes]
            imag = level_ref[
                pl.ds(pl.multiple_of((block * 2 + 1) * RADIX_A + start, 8), 8), lanes
            ]
            return turn((real, imag), turn_one_ref[0, q1, rows, :], turn_one_ref[1, q1, rows, :])

        first = []
        for b in range(8):
            four = dft4([load(8 * a + b) for a in range(4)], orient)
            first.append([spin(v, b * ja, orient) for ja, v in enumerate(four)])
        for ja in range(4):
            eight = dft8([first[b][ja] for b in range(8)], orient)
            for jb in range(8):
                j1 = ja + 4 * jb
                value = turn(eight[jb], turn_two_ref[0, j1], turn_two_ref[1, j1])
                out = pl.ds(pl.multiple_of(j1 * RADIX_A + start, 8), 8)
                turned_ref[out, :RADIX_C] = value[0]
                turned_ref[out, RADIX_C:] = value[1]
        return carry

    lax.fori_loop(0, RADIX_A // 8, group, 0)


def last(table_ref, turned_ref, store):
    step = 512
    for chunk in range(WIDE // step):
        block = turned_ref[chunk * step : (chunk + 1) * step, :].astype(BF16)
        store(
            slice(chunk * step, (chunk + 1) * step),
            lax.dot_general(
                table_ref[...], block, (((1,), (1,)), ((), ())), preferred_element_type=F32
            ),
        )


def compute_kernel(
    edges_ref,
    segment_ref,
    template_ref,
    first_fwd_ref,
    first_inv_ref,
    third_fwd_ref,
    third_inv_ref,
    turn_one_ref,
    turn_two_ref,
    snr_ref,
    chisq_ref,
    peak_ref,
    level_fwd_ref,
    level_inv_ref,
    turned_ref,
    corr_ref,
    piece_ref,
):
    level_fwd_ref[...] = jnp.dot(
        first_fwd_ref[...], segment_ref[...], preferred_element_type=F32
    )
    middle(level_fwd_ref, 8, -1, turn_one_ref, turn_two_ref, turned_ref)

    def keep_spectrum(lanes, value):
        corr_ref[:, lanes] = value

    last(third_fwd_ref, turned_ref, keep_spectrum)
    edges = [edges_ref[0, e] for e in range(3)]
    column = lax.broadcasted_iota(jnp.int32, (8, WIDE), 1)
    row = lax.broadcasted_iota(jnp.int32, (8, WIDE), 0)

    def correlate(s, sums):
        place = pl.multiple_of(s * 8, 8)
        both = template_ref[pl.ds(pl.multiple_of(s * 16, 16), 16), :].astype(F32)
        temp_real, temp_imag = both[:8], both[8:]
        upper = pl.ds(place, 8)
        lower = pl.ds(pl.multiple_of(RADIX_A + place, 8), 8)
        spec_real, spec_imag = corr_ref[upper, :], corr_ref[lower, :]
        corr_ref[upper, :] = spec_real * temp_real + spec_imag * temp_imag
        corr_ref[lower, :] = spec_imag * temp_real - spec_real * temp_imag
        power = temp_real * temp_real + temp_imag * temp_imag
        bins = (row + place) * WIDE + column

        def fold(values):
            return jnp.sum(values.reshape(8, WIDE // RADIX_C, RADIX_C), axis=1)

        above = [fold(jnp.where(bins >= edge, power, 0.0)) for edge in edges]
        parts = [fold(power)] + above
        return tuple(a + b for a, b in zip(sums, parts))

    zero = jnp.zeros((8, RADIX_C), F32)
    sums = lax.fori_loop(0, 8, correlate, (zero,) * 4)
    sums = [jnp.sum(v, axis=(0, 1), keepdims=True) for v in sums]
    total = sums[0]
    shares = [
        (sums[0] - sums[1]) / total,
        (sums[1] - sums[2]) / total,
        (sums[2] - sums[3]) / total,
        sums[3] / total,
    ]
    scale = float(LENGTH) / total

    def one_piece(number, carry):
        low = jnp.where(
            number == 0,
            0,
            jnp.where(number == 1, edges[0], jnp.where(number == 2, edges[1], edges[2])),
        )
        high = jnp.where(
            number == 0,
            edges[0],
            jnp.where(number == 1, edges[1], jnp.where(number == 2, edges[2], KEPT)),
        )
        step = 512
        for chunk in range(WIDE // step):
            lanes = slice(chunk * step, (chunk + 1) * step)
            shape = (2, RADIX_A, step)
            bins = (
                lax.broadcasted_iota(jnp.int32, shape, 1) * WIDE
                + lax.broadcasted_iota(jnp.int32, shape, 2)
                + chunk * step
            ).reshape(2 * RADIX_A, step)
            masked = jnp.where((bins >= low) & (bins < high), corr_ref[:, lanes], 0.0)
            level_inv_ref[:, lanes] = jnp.dot(
                first_inv_ref[...], masked.astype(BF16), preferred_element_type=F32
            )
        middle(level_inv_ref, 16, 1, turn_one_ref, turn_two_ref, turned_ref)

        def keep_piece(lanes, value):
            piece_ref[number, :, lanes] = value

        last(third_inv_ref, turned_ref, keep_piece)
        return carry

    lax.fori_loop(0, 4, one_piece, 0)

    def finish(t, best):
        rows = pl.ds(pl.multiple_of(t * 16, 16), 16)
        lower = pl.ds(pl.multiple_of(RADIX_A + t * 16, 16), 16)
        for chunk in range(WIDE // 512):
            lanes = slice(chunk * 512, (chunk + 1) * 512)
            real = [piece_ref[b, rows, lanes] for b in range(4)]
            imag = [piece_ref[b, lower, lanes] for b in range(4)]
            sum_real = real[0] + real[1] + real[2] + real[3]
            sum_imag = imag[0] + imag[1] + imag[2] + imag[3]
            snr = jnp.sqrt((sum_real * sum_real + sum_imag * sum_imag) * scale)
            chisq = jnp.zeros_like(snr)
            for b in range(4):
                diff_real = real[b] - shares[b] * sum_real
                diff_imag = imag[b] - shares[b] * sum_imag
                chisq = chisq + diff_real * diff_real + diff_imag * diff_imag
            chisq = chisq * scale
            reduced = chisq * (1.0 / 6.0)
            base = (1.0 + reduced * reduced * reduced) * 0.5
            weighted = snr * jnp.exp(jnp.log(base) * (-1.0 / 6.0))
            newsnr = jnp.where(reduced > 1.0, weighted, snr)
            snr_ref[rows, lanes] = snr.astype(BF16)
            chisq_ref[rows, lanes] = chisq.astype(BF16)
            for part in range(4):
                best = jnp.maximum(best, newsnr[:, part * RADIX_C : (part + 1) * RADIX_C])
        return best

    best = lax.fori_loop(0, 4, finish, jnp.zeros((16, RADIX_C), F32))
    peak_ref[...] = jnp.max(best, axis=(0, 1), keepdims=True)


def compute(edges, segment, template):
    vmem = pl.BlockSpec(memory_space=pltpu.VMEM)
    return pl.pallas_call(
        compute_kernel,
        out_shape=(
            jax.ShapeDtypeStruct((RADIX_A, WIDE), BF16),
            jax.ShapeDtypeStruct((RADIX_A, WIDE), BF16),
            jax.ShapeDtypeStruct((1, 1), F32),
        ),
        in_specs=[pl.BlockSpec(memory_space=pltpu.SMEM)] + [vmem] * 8,
        out_specs=(vmem, vmem, vmem),
        scratch_shapes=[
            pltpu.VMEM((SUBROWS * 2 * RADIX_A, INNER // SUBROWS), F32),
            pltpu.VMEM((4 * RADIX_A, WIDE), F32),
            pltpu.VMEM((WIDE, 2 * RADIX_C), F32),
            pltpu.VMEM((2 * RADIX_A, WIDE), F32),
            pltpu.VMEM((4, 2 * RADIX_A, WIDE), F32),
        ],
        compiler_params=pltpu.CompilerParams(vmem_limit_bytes=40 * 1024 * 1024),
    )(edges, segment, template, *[jnp.asarray(t) for t in tables()])


def move_general(strain_frames, frame_slot, templates):
    segments_count = lax.axis_size("segment")
    position = lax.axis_index("segment")
    frame_length = strain_frames.shape[1]
    counter = jnp.arange(segments_count, dtype=jnp.int32)
    slot_now = lax.dynamic_slice_in_dim(frame_slot, position, 1, 1)[:, 0]
    next_index = jnp.minimum(position + 1, segments_count - 1)
    slot_next = lax.dynamic_slice_in_dim(frame_slot, next_index, 1, 1)[:, 0]

    def arrange(slots, frames):
        selector = (counter[:, None] == slots[None, :]).astype(BF16)
        return jnp.dot(selector, frames, preferred_element_type=F32).astype(BF16).reshape(KEPT)

    following_rows = jnp.concatenate(
        [strain_frames[1:], jnp.zeros((1, frame_length), BF16)], axis=0
    )
    outgoing = jnp.stack([strain_frames, following_rows], axis=1)
    received = lax.all_to_all(outgoing, "segment", split_axis=0, concat_axis=0, tiled=True)
    leading = arrange(slot_now, received[:, 0])
    trailing = arrange(slot_next, received[:, 1])
    segment = jnp.concatenate([leading, trailing]).reshape(RADIX_A * SUBROWS, INNER // SUBROWS)
    whole = lax.all_gather(templates, "segment", axis=2, tiled=True)
    template = whole.reshape(2, 8, 8, WIDE).transpose(1, 0, 2, 3).reshape(2 * RADIX_A, WIDE)
    return segment, template


def local(strain_frames, frame_slot, templates, bin_edges):
    segment, template = move_general(strain_frames, frame_slot, templates)
    snr, chisq, peak = compute(bin_edges, segment, template)
    return (snr.reshape(1, 1, KEPT), chisq.reshape(1, 1, KEPT), peak)


def solution(mesh):
    in_specs = (
        P("segment", None),
        P(),
        P(("groups", "template"), None, "segment"),
        P(("groups", "template"), None),
    )
    out_specs = (
        P("segment", ("groups", "template"), None),
        P("segment", ("groups", "template"), None),
        P("segment", ("groups", "template")),
    )
    return jax.shard_map(local, mesh=mesh, in_specs=in_specs, out_specs=out_specs, check_vma=False)
```

```python
import functools
import functools
import math

import jax
import jax.numpy as jnp
import numpy as np
from jax import lax
from jax.experimental import pallas as pl
from jax.experimental.pallas import tpu as pltpu
from jax.sharding import PartitionSpec as P

RADIX_A = 64
RADIX_B = 32
RADIX_C = 128
LENGTH = RADIX_A * RADIX_B * RADIX_C
INNER = RADIX_B * RADIX_C
KEPT = LENGTH // 2
SUBROWS = 4
WIDE = INNER // 2
F32 = jnp.float32
BF16 = jnp.bfloat16


def dft_table(length, orient):
    counter = np.arange(length)
    angles = orient * 2.0 * math.pi / length * (counter[:, None] * counter[None, :] % length)
    cosine, sine = np.cos(angles), np.sin(angles)
    upper = np.stack([cosine, -sine], axis=1)
    lower = np.stack([sine, cosine], axis=1)
    return np.stack([upper, lower], axis=0).astype(np.float32)


def tables():
    base = dft_table(RADIX_A, -1.0)[:, :, 0, :]
    first_fwd = np.zeros((SUBROWS, 2, RADIX_A, RADIX_A, SUBROWS), np.float32)
    for sub in range(SUBROWS):
        first_fwd[sub, :, :, :, sub] = base
    first_fwd = first_fwd.reshape(SUBROWS * 2 * RADIX_A, RADIX_A * SUBROWS)
    base = dft_table(RADIX_A, 1.0)[:, :, :, : RADIX_A // 2]
    first_inv = np.zeros((2, 2, RADIX_A, 2, RADIX_A // 2, 2), np.float32)
    for half in range(2):
        first_inv[half, :, :, :, :, half] = base
    first_inv = first_inv.reshape(4 * RADIX_A, 2 * RADIX_A)
    third_fwd = dft_table(RADIX_C, -1.0)[:, : RADIX_C // 2].reshape(RADIX_C, 2 * RADIX_C)
    low = RADIX_C // 4
    third_inv = dft_table(RADIX_C, 1.0)[:, low : low + RADIX_C // 2].reshape(RADIX_C, 2 * RADIX_C)
    third_inv = third_inv.astype(BF16).astype(np.float32) / LENGTH
    k1 = np.arange(RADIX_A)[None, :, None]
    q1 = np.arange(RADIX_B)[:, None, None]
    q2 = np.arange(RADIX_C)[None, None, :]
    angle = 2.0 * math.pi / LENGTH * (k1 * (RADIX_C * q1 + q2) % LENGTH)
    turn_one = np.stack([np.cos(angle), np.sin(angle)]).astype(np.float32)
    angle = 2.0 * math.pi / INNER * (q1 * q2 % INNER)
    turn_two = np.stack([np.cos(angle), np.sin(angle)]).astype(np.float32)
    turn_two = np.broadcast_to(turn_two, (2, RADIX_B, 8, RADIX_C)).copy()
    return (
        first_fwd.astype(BF16),
        first_inv.astype(BF16),
        third_fwd.astype(BF16),
        third_inv.astype(BF16),
        turn_one,
        turn_two,
    )


def cadd(a, b):
    return (a[0] + b[0], a[1] + b[1])


def csub(a, b):
    return (a[0] - b[0], a[1] - b[1])


def quarter(a, orient):
    return (-a[1], a[0]) if orient > 0 else (a[1], -a[0])


def spin(a, eighths, orient):
    eighths = eighths % 32
    if eighths == 0:
        return a
    if eighths == 8:
        return quarter(a, orient)
    if eighths == 4:
        root = math.sqrt(0.5)
        b = quarter(a, orient)
        return ((a[0] + b[0]) * root, (a[1] + b[1]) * root)
    angle = orient * 2.0 * math.pi * eighths / 32
    cosine, sine = math.cos(angle), math.sin(angle)
    return (a[0] * cosine - a[1] * sine, a[0] * sine + a[1] * cosine)


def dft4(x, orient):
    a, b = cadd(x[0], x[2]), csub(x[0], x[2])
    c, d = cadd(x[1], x[3]), quarter(csub(x[1], x[3]), orient)
    return [cadd(a, c), cadd(b, d), csub(a, c), csub(b, d)]


def dft8(x, orient):
    even = dft4(x[0::2], orient)
    odd = dft4(x[1::2], orient)
    odd = [spin(v, 4 * k, orient) for k, v in enumerate(odd)]
    return [cadd(e, o) for e, o in zip(even, odd)] + [csub(e, o) for e, o in zip(even, odd)]


def middle(level_ref, per_row, orient, turn_one_ref, turn_two_ref, turned_ref):
    def turn(value, cosine, sine):
        if orient < 0:
            return (value[0] * cosine + value[1] * sine, value[1] * cosine - value[0] * sine)
        return (value[0] * cosine - value[1] * sine, value[0] * sine + value[1] * cosine)

    def group(g, carry):
        start = pl.multiple_of(g * 8, 8)
        rows = pl.ds(start, 8)

        def load(q1):
            block, lane = q1 // per_row, (q1 % per_row) * RADIX_C
            lanes = slice(lane, lane + RADIX_C)
            real = level_ref[pl.ds(pl.multiple_of(block * 2 * RADIX_A + start, 8), 8), lanes]
            imag = level_ref[
                pl.ds(pl.multiple_of((block * 2 + 1) * RADIX_A + start, 8), 8), lanes
            ]
            return turn((real, imag), turn_one_ref[0, q1, rows, :], turn_one_ref[1, q1, rows, :])

        first = []
        for b in range(8):
            four = dft4([load(8 * a + b) for a in range(4)], orient)
            first.append([spin(v, b * ja, orient) for ja, v in enumerate(four)])
        for ja in range(4):
            eight = dft8([first[b][ja] for b in range(8)], orient)
            for jb in range(8):
                j1 = ja + 4 * jb
                value = turn(eight[jb], turn_two_ref[0, j1], turn_two_ref[1, j1])
                out = pl.ds(pl.multiple_of(j1 * RADIX_A + start, 8), 8)
                turned_ref[out, :RADIX_C] = value[0]
                turned_ref[out, RADIX_C:] = value[1]
        return carry

    lax.fori_loop(0, RADIX_A // 8, group, 0)


def last(table_ref, turned_ref, store):
    step = 512
    for chunk in range(WIDE // step):
        block = turned_ref[chunk * step : (chunk + 1) * step, :].astype(BF16)
        store(
            slice(chunk * step, (chunk + 1) * step),
            lax.dot_general(
                table_ref[...], block, (((1,), (1,)), ((), ())), preferred_element_type=F32
            ),
        )


def compute_kernel(
    edges_ref,
    slot_ref,
    received_ref,
    template_ref,
    first_fwd_ref,
    first_inv_ref,
    third_fwd_ref,
    third_inv_ref,
    turn_one_ref,
    turn_two_ref,
    snr_ref,
    chisq_ref,
    peak_ref,
    level_fwd_ref,
    level_inv_ref,
    turned_ref,
    corr_ref,
    piece_ref,
    segment_ref,
    in_order,
):
    if in_order:
        segment_ref = received_ref
    else:
        position = lax.axis_index("segment")
        for kind in range(2):
            half = jnp.minimum(position + kind, 7)
            for source in range(8):
                place = pl.multiple_of((kind * 8 + slot_ref[source, half]) * 16, 16)
                begin = (kind * 8 + source) * 16
                segment_ref[pl.ds(place, 16), :] = received_ref[begin : begin + 16, :]
    level_fwd_ref[...] = jnp.dot(
        first_fwd_ref[...], segment_ref[...], preferred_element_type=F32
    )
    middle(level_fwd_ref, 8, -1, turn_one_ref, turn_two_ref, turned_ref)

    def keep_spectrum(lanes, value):
        corr_ref[:, lanes] = value

    last(third_fwd_ref, turned_ref, keep_spectrum)
    edges = [edges_ref[0, e] for e in range(3)]
    column = lax.broadcasted_iota(jnp.int32, (8, WIDE), 1)
    row = lax.broadcasted_iota(jnp.int32, (8, WIDE), 0)

    def correlate(s, sums):
        place = pl.multiple_of(s * 8, 8)
        both = template_ref[pl.ds(pl.multiple_of(s * 16, 16), 16), :].astype(F32)
        temp_real, temp_imag = both[:8], both[8:]
        upper = pl.ds(place, 8)
        lower = pl.ds(pl.multiple_of(RADIX_A + place, 8), 8)
        spec_real, spec_imag = corr_ref[upper, :], corr_ref[lower, :]
        corr_ref[upper, :] = spec_real * temp_real + spec_imag * temp_imag
        corr_ref[lower, :] = spec_imag * temp_real - spec_real * temp_imag
        power = temp_real * temp_real + temp_imag * temp_imag
        bins = (row + place) * WIDE + column

        def fold(values):
            return jnp.sum(values.reshape(8, WIDE // RADIX_C, RADIX_C), axis=1)

        above = [fold(jnp.where(bins >= edge, power, 0.0)) for edge in edges]
        parts = [fold(power)] + above
        return tuple(a + b for a, b in zip(sums, parts))

    zero = jnp.zeros((8, RADIX_C), F32)
    sums = lax.fori_loop(0, 8, correlate, (zero,) * 4)
    sums = [jnp.sum(v, axis=(0, 1), keepdims=True) for v in sums]
    total = sums[0]
    shares = [
        (sums[0] - sums[1]) / total,
        (sums[1] - sums[2]) / total,
        (sums[2] - sums[3]) / total,
        sums[3] / total,
    ]
    scale = float(LENGTH) / total

    def one_piece(number, carry):
        low = jnp.where(
            number == 0,
            0,
            jnp.where(number == 1, edges[0], jnp.where(number == 2, edges[1], edges[2])),
        )
        high = jnp.where(
            number == 0,
            edges[0],
            jnp.where(number == 1, edges[1], jnp.where(number == 2, edges[2], KEPT)),
        )
        step = 512
        for chunk in range(WIDE // step):
            lanes = slice(chunk * step, (chunk + 1) * step)
            shape = (2, RADIX_A, step)
            bins = (
                lax.broadcasted_iota(jnp.int32, shape, 1) * WIDE
                + lax.broadcasted_iota(jnp.int32, shape, 2)
                + chunk * step
            ).reshape(2 * RADIX_A, step)
            masked = jnp.where((bins >= low) & (bins < high), corr_ref[:, lanes], 0.0)
            level_inv_ref[:, lanes] = jnp.dot(
                first_inv_ref[...], masked.astype(BF16), preferred_element_type=F32
            )
        middle(level_inv_ref, 16, 1, turn_one_ref, turn_two_ref, turned_ref)

        def keep_piece(lanes, value):
            piece_ref[number, :, lanes] = value

        last(third_inv_ref, turned_ref, keep_piece)
        return carry

    lax.fori_loop(0, 4, one_piece, 0)

    def finish(t, best):
        rows = pl.ds(pl.multiple_of(t * 16, 16), 16)
        lower = pl.ds(pl.multiple_of(RADIX_A + t * 16, 16), 16)
        for chunk in range(WIDE // 512):
            lanes = slice(chunk * 512, (chunk + 1) * 512)
            real = [piece_ref[b, rows, lanes] for b in range(4)]
            imag = [piece_ref[b, lower, lanes] for b in range(4)]
            sum_real = real[0] + real[1] + real[2] + real[3]
            sum_imag = imag[0] + imag[1] + imag[2] + imag[3]
            snr = jnp.sqrt((sum_real * sum_real + sum_imag * sum_imag) * scale)
            chisq = jnp.zeros_like(snr)
            for b in range(4):
                diff_real = real[b] - shares[b] * sum_real
                diff_imag = imag[b] - shares[b] * sum_imag
                chisq = chisq + diff_real * diff_real + diff_imag * diff_imag
            chisq = chisq * scale
            reduced = chisq * (1.0 / 6.0)
            base = (1.0 + reduced * reduced * reduced) * 0.5
            weighted = snr * jnp.exp(jnp.log(base) * (-1.0 / 6.0))
            newsnr = jnp.where(reduced > 1.0, weighted, snr)
            snr_ref[rows, lanes] = snr.astype(BF16)
            chisq_ref[rows, lanes] = chisq.astype(BF16)
            for part in range(4):
                best = jnp.maximum(best, newsnr[:, part * RADIX_C : (part + 1) * RADIX_C])
        return best

    best = lax.fori_loop(0, 4, finish, jnp.zeros((16, RADIX_C), F32))
    peak_ref[...] = jnp.max(best, axis=(0, 1), keepdims=True)


def compute(edges, slots, segment, template, in_order):
    vmem = pl.BlockSpec(memory_space=pltpu.VMEM)
    smem = pl.BlockSpec(memory_space=pltpu.SMEM)
    return pl.pallas_call(
        functools.partial(compute_kernel, in_order=in_order),
        out_shape=(
            jax.ShapeDtypeStruct((RADIX_A, WIDE), BF16),
            jax.ShapeDtypeStruct((RADIX_A, WIDE), BF16),
            jax.ShapeDtypeStruct((1, 1), F32),
        ),
        in_specs=[smem] * 2 + [vmem] * 8,
        out_specs=(vmem, vmem, vmem),
        scratch_shapes=[
            pltpu.VMEM((SUBROWS * 2 * RADIX_A, INNER // SUBROWS), F32),
            pltpu.VMEM((4 * RADIX_A, WIDE), F32),
            pltpu.VMEM((WIDE, 2 * RADIX_C), F32),
            pltpu.VMEM((2 * RADIX_A, WIDE), F32),
            pltpu.VMEM((4, 2 * RADIX_A, WIDE), F32),
            pltpu.VMEM((RADIX_A * SUBROWS, INNER // SUBROWS), BF16),
        ],
        compiler_params=pltpu.CompilerParams(vmem_limit_bytes=40 * 1024 * 1024),
    )(edges, slots, segment, template, *[jnp.asarray(t) for t in tables()])


def move_general(strain_frames, frame_slot, templates):
    segments_count = lax.axis_size("segment")
    position = lax.axis_index("segment")
    frame_length = strain_frames.shape[1]
    counter = jnp.arange(segments_count, dtype=jnp.int32)
    slot_now = lax.dynamic_slice_in_dim(frame_slot, position, 1, 1)[:, 0]
    next_index = jnp.minimum(position + 1, segments_count - 1)
    slot_next = lax.dynamic_slice_in_dim(frame_slot, next_index, 1, 1)[:, 0]

    def arrange(slots, frames):
        selector = (counter[:, None] == slots[None, :]).astype(BF16)
        return jnp.dot(selector, frames, preferred_element_type=F32).astype(BF16).reshape(KEPT)

    following_rows = jnp.concatenate(
        [strain_frames[1:], jnp.zeros((1, frame_length), BF16)], axis=0
    )
    outgoing = jnp.stack([strain_frames, following_rows], axis=1)
    received = lax.all_to_all(outgoing, "segment", split_axis=0, concat_axis=0, tiled=True)
    leading = arrange(slot_now, received[:, 0])
    trailing = arrange(slot_next, received[:, 1])
    segment = jnp.concatenate([leading, trailing]).reshape(RADIX_A * SUBROWS, INNER // SUBROWS)
    whole = lax.all_gather(templates, "segment", axis=2, tiled=True)
    template = whole.reshape(2, 8, 8, WIDE).transpose(1, 0, 2, 3).reshape(2 * RADIX_A, WIDE)
    return segment, template


def move_kernel(frames_ref, block_ref, frames_out, blocks_out, local_sem, send, recv):
    me = lax.axis_index("segment")
    core = lax.axis_index("template")
    other = {"template": 1 - core}
    beside = {"segment": me + 1 - 2 * (me % 2)}

    def after(step):
        return (me + step) % 8

    barrier = pltpu.get_barrier_semaphore()
    for step in range(1, 8):
        pl.semaphore_signal(
            barrier, inc=1, device_id={"segment": after(step)}, device_id_type=pl.DeviceIdType.MESH
        )
    pl.semaphore_signal(barrier, inc=1, device_id=other, device_id_type=pl.DeviceIdType.MESH)
    pl.semaphore_wait(barrier, 8)

    def remote(source, target, row, step, device):
        return pltpu.make_async_remote_copy(
            src_ref=source,
            dst_ref=target,
            send_sem=send.at[row, step],
            recv_sem=recv.at[row, step],
            device_id=device,
            device_id_type=pl.DeviceIdType.MESH,
        )

    own_frame = frames_ref.at[me + core]
    local_frame = pltpu.make_async_copy(own_frame, frames_out.at[core, me], local_sem.at[0])
    local_block = pltpu.make_async_copy(block_ref, blocks_out.at[me], local_sem.at[1])
    sends = []

    def begin(copy):
        copy.start()
        sends.append(copy)

    for step in FAR_FIRST:
        there = after(step)
        begin(
            remote(
                frames_ref.at[there + core],
                frames_out.at[core, me],
                0,
                step,
                {"segment": there},
            )
        )
        if step % 2 == 0:
            begin(remote(block_ref, blocks_out.at[me], 2, step, {"segment": there}))
    begin(remote(own_frame, frames_out.at[core, me], 1, 0, other))
    begin(remote(block_ref, blocks_out.at[me], 3, 0, beside))
    local_frame.start()
    local_block.start()
    for step in NEAR_FIRST:
        source = after(8 - step)
        slot = frames_out.at[core, source]
        remote(slot, slot, 0, step, {"segment": source}).wait_recv()
        begin(remote(slot, slot, 1, step, other))
        if step % 2 == 0:
            slot = blocks_out.at[source]
            remote(slot, slot, 2, step, {"segment": source}).wait_recv()
            begin(remote(slot, slot, 3, step, beside))
    local_frame.wait()
    local_block.wait()
    neighbour = me + 1 - 2 * (me % 2)
    for step in range(8):
        slot = frames_out.at[1 - core, after(8 - step)]
        remote(slot, slot, 1, step, other).wait_recv()
        if step % 2 == 0:
            slot = blocks_out.at[(neighbour + 8 - step) % 8]
            remote(slot, slot, 3, step, beside).wait_recv()
    for copy in sends:
        copy.wait_send()


FAR_FIRST = (4, 6, 2, 5, 3, 7, 1)
NEAR_FIRST = (1, 7, 2, 6, 3, 5, 4)


def move(strain_frames, templates):
    frames = jnp.concatenate(
        [strain_frames.reshape(8, 16, 1024), jnp.zeros((1, 16, 1024), BF16)], axis=0
    )
    block = templates.reshape(16, WIDE)
    anywhere = pl.BlockSpec(memory_space=pl.ANY)
    received, blocks = pl.pallas_call(
        move_kernel,
        out_shape=(
            jax.ShapeDtypeStruct((2, 8, 16, 1024), BF16),
            jax.ShapeDtypeStruct((8, 16, WIDE), BF16),
        ),
        in_specs=[anywhere, anywhere],
        out_specs=(anywhere, anywhere),
        scratch_shapes=[
            pltpu.SemaphoreType.DMA((2,)),
            pltpu.SemaphoreType.DMA((4, 8)),
            pltpu.SemaphoreType.DMA((4, 8)),
        ],
        compiler_params=pltpu.CompilerParams(collective_id=0, has_side_effects=True),
    )(frames, block)
    return received.reshape(256, 1024), blocks.reshape(2 * RADIX_A, WIDE)


def local(strain_frames, frame_slot, templates, bin_edges):
    direct = lax.axis_size("segment") == 8 and strain_frames.shape[1] == 16384
    if direct:
        segment, template = move(strain_frames, templates)
    else:
        segment, template = move_general(strain_frames, frame_slot, templates)
    snr, chisq, peak = compute(bin_edges, frame_slot, segment, template, not direct)
    return (snr.reshape(1, 1, KEPT), chisq.reshape(1, 1, KEPT), peak)


def solution(mesh):
    in_specs = (
        P("segment", None),
        P(),
        P(("groups", "template"), None, "segment"),
        P(("groups", "template"), None),
    )
    out_specs = (
        P("segment", ("groups", "template"), None),
        P("segment", ("groups", "template"), None),
        P("segment", ("groups", "template")),
    )
    return jax.shard_map(local, mesh=mesh, in_specs=in_specs, out_specs=out_specs, check_vma=False)
```

```python
import functools
import functools
import math

import jax
import jax.numpy as jnp
import numpy as np
from jax import lax
from jax.experimental import pallas as pl
from jax.experimental.pallas import tpu as pltpu
from jax.sharding import PartitionSpec as P

RADIX_A = 64
RADIX_B = 32
RADIX_C = 128
LENGTH = RADIX_A * RADIX_B * RADIX_C
INNER = RADIX_B * RADIX_C
KEPT = LENGTH // 2
SUBROWS = 4
WIDE = INNER // 2
F32 = jnp.float32
BF16 = jnp.bfloat16


def dft_table(length, orient):
    counter = np.arange(length)
    angles = orient * 2.0 * math.pi / length * (counter[:, None] * counter[None, :] % length)
    cosine, sine = np.cos(angles), np.sin(angles)
    upper = np.stack([cosine, -sine], axis=1)
    lower = np.stack([sine, cosine], axis=1)
    return np.stack([upper, lower], axis=0).astype(np.float32)


def tables():
    base = dft_table(RADIX_A, -1.0)[:, :, 0, :]
    first_fwd = np.zeros((SUBROWS, 2, RADIX_A, RADIX_A, SUBROWS), np.float32)
    for sub in range(SUBROWS):
        first_fwd[sub, :, :, :, sub] = base
    first_fwd = first_fwd.reshape(SUBROWS * 2 * RADIX_A, RADIX_A * SUBROWS)
    base = dft_table(RADIX_A, 1.0)[:, :, :, : RADIX_A // 2]
    first_inv = np.zeros((2, 2, RADIX_A, 2, RADIX_A // 2, 2), np.float32)
    for half in range(2):
        first_inv[half, :, :, :, :, half] = base
    first_inv = first_inv.reshape(4 * RADIX_A, 2 * RADIX_A)
    third_fwd = dft_table(RADIX_C, -1.0)[:, : RADIX_C // 2].reshape(RADIX_C, 2 * RADIX_C)
    low = RADIX_C // 4
    third_inv = dft_table(RADIX_C, 1.0)[:, low : low + RADIX_C // 2].reshape(RADIX_C, 2 * RADIX_C)
    third_inv = third_inv.astype(BF16).astype(np.float32) / LENGTH
    k1 = np.arange(RADIX_A)[None, :, None]
    q1 = np.arange(RADIX_B)[:, None, None]
    q2 = np.arange(RADIX_C)[None, None, :]
    angle = 2.0 * math.pi / LENGTH * (k1 * (RADIX_C * q1 + q2) % LENGTH)
    turn_one = np.stack([np.cos(angle), np.sin(angle)]).astype(np.float32)
    angle = 2.0 * math.pi / INNER * (q1 * q2 % INNER)
    turn_two = np.stack([np.cos(angle), np.sin(angle)]).astype(np.float32)
    turn_two = np.broadcast_to(turn_two, (2, RADIX_B, 8, RADIX_C)).copy()
    return (
        first_fwd.astype(BF16),
        first_inv.astype(BF16),
        third_fwd.astype(BF16),
        third_inv.astype(BF16),
        turn_one,
        turn_two,
    )


def cadd(a, b):
    return (a[0] + b[0], a[1] + b[1])


def csub(a, b):
    return (a[0] - b[0], a[1] - b[1])


def quarter(a, orient):
    return (-a[1], a[0]) if orient > 0 else (a[1], -a[0])


def spin(a, eighths, orient):
    eighths = eighths % 32
    if eighths == 0:
        return a
    if eighths == 8:
        return quarter(a, orient)
    if eighths == 4:
        root = math.sqrt(0.5)
        b = quarter(a, orient)
        return ((a[0] + b[0]) * root, (a[1] + b[1]) * root)
    angle = orient * 2.0 * math.pi * eighths / 32
    cosine, sine = math.cos(angle), math.sin(angle)
    return (a[0] * cosine - a[1] * sine, a[0] * sine + a[1] * cosine)


def dft4(x, orient):
    a, b = cadd(x[0], x[2]), csub(x[0], x[2])
    c, d = cadd(x[1], x[3]), quarter(csub(x[1], x[3]), orient)
    return [cadd(a, c), cadd(b, d), csub(a, c), csub(b, d)]


def dft8(x, orient):
    even = dft4(x[0::2], orient)
    odd = dft4(x[1::2], orient)
    odd = [spin(v, 4 * k, orient) for k, v in enumerate(odd)]
    return [cadd(e, o) for e, o in zip(even, odd)] + [csub(e, o) for e, o in zip(even, odd)]


def middle(level_ref, per_row, orient, turn_one_ref, turn_two_ref, turned_ref):
    def turn(value, cosine, sine):
        if orient < 0:
            return (value[0] * cosine + value[1] * sine, value[1] * cosine - value[0] * sine)
        return (value[0] * cosine - value[1] * sine, value[0] * sine + value[1] * cosine)

    def group(g, carry):
        start = pl.multiple_of(g * 8, 8)
        rows = pl.ds(start, 8)

        def load(q1):
            block, lane = q1 // per_row, (q1 % per_row) * RADIX_C
            lanes = slice(lane, lane + RADIX_C)
            real = level_ref[pl.ds(pl.multiple_of(block * 2 * RADIX_A + start, 8), 8), lanes]
            imag = level_ref[
                pl.ds(pl.multiple_of((block * 2 + 1) * RADIX_A + start, 8), 8), lanes
            ]
            return turn((real, imag), turn_one_ref[0, q1, rows, :], turn_one_ref[1, q1, rows, :])

        first = []
        for b in range(8):
            four = dft4([load(8 * a + b) for a in range(4)], orient)
            first.append([spin(v, b * ja, orient) for ja, v in enumerate(four)])
        for ja in range(4):
            eight = dft8([first[b][ja] for b in range(8)], orient)
            for jb in range(8):
                j1 = ja + 4 * jb
                value = turn(eight[jb], turn_two_ref[0, j1], turn_two_ref[1, j1])
                out = pl.ds(pl.multiple_of(j1 * RADIX_A + start, 8), 8)
                turned_ref[out, :RADIX_C] = value[0]
                turned_ref[out, RADIX_C:] = value[1]
        return carry

    lax.fori_loop(0, RADIX_A // 8, group, 0)


def last(table_ref, turned_ref, store):
    step = 512
    for chunk in range(WIDE // step):
        block = turned_ref[chunk * step : (chunk + 1) * step, :].astype(BF16)
        store(
            slice(chunk * step, (chunk + 1) * step),
            lax.dot_general(
                table_ref[...], block, (((1,), (1,)), ((), ())), preferred_element_type=F32
            ),
        )


def compute_kernel(edges_ref, slot_ref, *refs, in_order):
    sources, refs = refs[:8], refs[8:]
    snr_ref, chisq_ref, peak_ref = refs[:3]
    level_fwd_ref, level_inv_ref, turned_ref, corr_ref, piece_ref, segment_ref = refs[3:9]
    places, fetch_sem = refs[9:17], refs[17]
    fetches = [
        pltpu.make_async_copy(source, place, fetch_sem.at[number])
        for number, (source, place) in enumerate(zip(sources, places))
    ]
    for number in (0, 2, 6, 7, 4, 1, 3, 5):
        fetches[number].start()
    received_ref, template_ref, first_fwd_ref, first_inv_ref = places[:4]
    third_fwd_ref, third_inv_ref, turn_one_ref, turn_two_ref = places[4:]
    fetches[0].wait()
    if in_order:
        segment_ref = received_ref
    else:
        position = lax.axis_index("segment")
        for kind in range(2):
            half = jnp.minimum(position + kind, 7)
            for source in range(8):
                place = pl.multiple_of((kind * 8 + slot_ref[source, half]) * 16, 16)
                begin = (kind * 8 + source) * 16
                segment_ref[pl.ds(place, 16), :] = received_ref[begin : begin + 16, :]
    fetches[2].wait()
    level_fwd_ref[...] = jnp.dot(
        first_fwd_ref[...], segment_ref[...], preferred_element_type=F32
    )
    fetches[6].wait()
    fetches[7].wait()
    middle(level_fwd_ref, 8, -1, turn_one_ref, turn_two_ref, turned_ref)

    def keep_spectrum(lanes, value):
        corr_ref[:, lanes] = value

    fetches[4].wait()
    last(third_fwd_ref, turned_ref, keep_spectrum)
    for number in (1, 3, 5):
        fetches[number].wait()
    edges = [edges_ref[0, e] for e in range(3)]
    column = lax.broadcasted_iota(jnp.int32, (8, WIDE), 1)
    row = lax.broadcasted_iota(jnp.int32, (8, WIDE), 0)

    def correlate(s, sums):
        place = pl.multiple_of(s * 8, 8)
        both = template_ref[pl.ds(pl.multiple_of(s * 16, 16), 16), :].astype(F32)
        temp_real, temp_imag = both[:8], both[8:]
        upper = pl.ds(place, 8)
        lower = pl.ds(pl.multiple_of(RADIX_A + place, 8), 8)
        spec_real, spec_imag = corr_ref[upper, :], corr_ref[lower, :]
        corr_ref[upper, :] = spec_real * temp_real + spec_imag * temp_imag
        corr_ref[lower, :] = spec_imag * temp_real - spec_real * temp_imag
        power = temp_real * temp_real + temp_imag * temp_imag
        bins = (row + place) * WIDE + column

        def fold(values):
            return jnp.sum(values.reshape(8, WIDE // RADIX_C, RADIX_C), axis=1)

        above = [fold(jnp.where(bins >= edge, power, 0.0)) for edge in edges]
        parts = [fold(power)] + above
        return tuple(a + b for a, b in zip(sums, parts))

    zero = jnp.zeros((8, RADIX_C), F32)
    sums = lax.fori_loop(0, 8, correlate, (zero,) * 4)
    sums = [jnp.sum(v, axis=(0, 1), keepdims=True) for v in sums]
    total = sums[0]
    shares = [
        (sums[0] - sums[1]) / total,
        (sums[1] - sums[2]) / total,
        (sums[2] - sums[3]) / total,
        sums[3] / total,
    ]
    scale = float(LENGTH) / total

    def one_piece(number, carry):
        low = jnp.where(
            number == 0,
            0,
            jnp.where(number == 1, edges[0], jnp.where(number == 2, edges[1], edges[2])),
        )
        high = jnp.where(
            number == 0,
            edges[0],
            jnp.where(number == 1, edges[1], jnp.where(number == 2, edges[2], KEPT)),
        )
        step = 512
        for chunk in range(WIDE // step):
            lanes = slice(chunk * step, (chunk + 1) * step)
            shape = (2, RADIX_A, step)
            bins = (
                lax.broadcasted_iota(jnp.int32, shape, 1) * WIDE
                + lax.broadcasted_iota(jnp.int32, shape, 2)
                + chunk * step
            ).reshape(2 * RADIX_A, step)
            masked = jnp.where((bins >= low) & (bins < high), corr_ref[:, lanes], 0.0)
            level_inv_ref[:, lanes] = jnp.dot(
                first_inv_ref[...], masked.astype(BF16), preferred_element_type=F32
            )
        middle(level_inv_ref, 16, 1, turn_one_ref, turn_two_ref, turned_ref)

        def keep_piece(lanes, value):
            piece_ref[number, :, lanes] = value

        last(third_inv_ref, turned_ref, keep_piece)
        return carry

    lax.fori_loop(0, 4, one_piece, 0)

    def finish(t, best):
        rows = pl.ds(pl.multiple_of(t * 16, 16), 16)
        lower = pl.ds(pl.multiple_of(RADIX_A + t * 16, 16), 16)
        for chunk in range(WIDE // 512):
            lanes = slice(chunk * 512, (chunk + 1) * 512)
            real = [piece_ref[b, rows, lanes] for b in range(4)]
            imag = [piece_ref[b, lower, lanes] for b in range(4)]
            sum_real = real[0] + real[1] + real[2] + real[3]
            sum_imag = imag[0] + imag[1] + imag[2] + imag[3]
            snr = jnp.sqrt((sum_real * sum_real + sum_imag * sum_imag) * scale)
            chisq = jnp.zeros_like(snr)
            for b in range(4):
                diff_real = real[b] - shares[b] * sum_real
                diff_imag = imag[b] - shares[b] * sum_imag
                chisq = chisq + diff_real * diff_real + diff_imag * diff_imag
            chisq = chisq * scale
            reduced = chisq * (1.0 / 6.0)
            base = (1.0 + reduced * reduced * reduced) * 0.5
            weighted = snr * jnp.exp(jnp.log(base) * (-1.0 / 6.0))
            newsnr = jnp.where(reduced > 1.0, weighted, snr)
            snr_ref[rows, lanes] = snr.astype(BF16)
            chisq_ref[rows, lanes] = chisq.astype(BF16)
            for part in range(4):
                best = jnp.maximum(best, newsnr[:, part * RADIX_C : (part + 1) * RADIX_C])
        return best

    best = lax.fori_loop(0, 4, finish, jnp.zeros((16, RADIX_C), F32))
    peak_ref[...] = jnp.max(best, axis=(0, 1), keepdims=True)


def compute(edges, slots, segment, template, in_order):
    vmem = pl.BlockSpec(memory_space=pltpu.VMEM)
    smem = pl.BlockSpec(memory_space=pltpu.SMEM)
    operands = [segment, template] + [jnp.asarray(t) for t in tables()]
    return pl.pallas_call(
        functools.partial(compute_kernel, in_order=in_order),
        out_shape=(
            jax.ShapeDtypeStruct((RADIX_A, WIDE), BF16),
            jax.ShapeDtypeStruct((RADIX_A, WIDE), BF16),
            jax.ShapeDtypeStruct((1, 1), F32),
        ),
        in_specs=[smem] * 2 + [pl.BlockSpec(memory_space=pltpu.HBM)] * 8,
        out_specs=(vmem, vmem, vmem),
        scratch_shapes=[
            pltpu.VMEM((SUBROWS * 2 * RADIX_A, INNER // SUBROWS), F32),
            pltpu.VMEM((4 * RADIX_A, WIDE), F32),
            pltpu.VMEM((WIDE, 2 * RADIX_C), F32),
            pltpu.VMEM((2 * RADIX_A, WIDE), F32),
            pltpu.VMEM((4, 2 * RADIX_A, WIDE), F32),
            pltpu.VMEM((RADIX_A * SUBROWS, INNER // SUBROWS), BF16),
        ]
        + [pltpu.VMEM(operand.shape, operand.dtype) for operand in operands]
        + [pltpu.SemaphoreType.DMA((8,))],
        compiler_params=pltpu.CompilerParams(vmem_limit_bytes=40 * 1024 * 1024),
    )(edges, slots, *operands)


def move_general(strain_frames, frame_slot, templates):
    segments_count = lax.axis_size("segment")
    position = lax.axis_index("segment")
    frame_length = strain_frames.shape[1]
    counter = jnp.arange(segments_count, dtype=jnp.int32)
    slot_now = lax.dynamic_slice_in_dim(frame_slot, position, 1, 1)[:, 0]
    next_index = jnp.minimum(position + 1, segments_count - 1)
    slot_next = lax.dynamic_slice_in_dim(frame_slot, next_index, 1, 1)[:, 0]

    def arrange(slots, frames):
        selector = (counter[:, None] == slots[None, :]).astype(BF16)
        return jnp.dot(selector, frames, preferred_element_type=F32).astype(BF16).reshape(KEPT)

    following_rows = jnp.concatenate(
        [strain_frames[1:], jnp.zeros((1, frame_length), BF16)], axis=0
    )
    outgoing = jnp.stack([strain_frames, following_rows], axis=1)
    received = lax.all_to_all(outgoing, "segment", split_axis=0, concat_axis=0, tiled=True)
    leading = arrange(slot_now, received[:, 0])
    trailing = arrange(slot_next, received[:, 1])
    segment = jnp.concatenate([leading, trailing]).reshape(RADIX_A * SUBROWS, INNER // SUBROWS)
    whole = lax.all_gather(templates, "segment", axis=2, tiled=True)
    template = whole.reshape(2, 8, 8, WIDE).transpose(1, 0, 2, 3).reshape(2 * RADIX_A, WIDE)
    return segment, template


def move_kernel(
    strain_ref,
    template_ref,
    frames_out,
    blocks_out,
    wide_ref,
    frames_ref,
    block_ref,
    local_sem,
    send,
    recv,
):
    me = lax.axis_index("segment")
    core = lax.axis_index("template")
    other = {"template": 1 - core}

    def after(step):
        return (me + step) % 8

    barrier = pltpu.get_barrier_semaphore()
    for step in range(1, 8):
        pl.semaphore_signal(
            barrier, inc=1, device_id={"segment": after(step)}, device_id_type=pl.DeviceIdType.MESH
        )
    pl.semaphore_signal(barrier, inc=1, device_id=other, device_id_type=pl.DeviceIdType.MESH)
    parts = [template_ref[0, :, row * WIDE : (row + 1) * WIDE].astype(F32) for row in range(8)]
    rows = [p[c : c + 1] for c in range(2) for p in parts]
    block_ref[...] = jnp.concatenate(rows, axis=0).astype(BF16)
    for row in range(16):
        wide_ref[:, row, :] = strain_ref[:, row * 1024 : (row + 1) * 1024].astype(F32)
    for frame in range(8):
        frames_ref[frame] = wide_ref[frame].astype(BF16)
    frames_ref[8] = jnp.zeros((16, 1024), BF16)
    pl.semaphore_wait(barrier, 8)

    def remote(source, target, row, step, device):
        return pltpu.make_async_remote_copy(
            src_ref=source,
            dst_ref=target,
            send_sem=send.at[row, step],
            recv_sem=recv.at[row, step],
            device_id=device,
            device_id_type=pl.DeviceIdType.MESH,
        )

    own_frame = frames_ref.at[me + core]
    local_frame = pltpu.make_async_copy(own_frame, frames_out.at[core, me], local_sem.at[0])
    local_block = pltpu.make_async_copy(block_ref, blocks_out.at[me], local_sem.at[1])
    sends = []

    def begin(copy):
        copy.start()
        sends.append(copy)

    for step in FAR_FIRST:
        there = after(step)
        begin(
            remote(
                frames_ref.at[there + core],
                frames_out.at[core, me],
                0,
                step,
                {"segment": there},
            )
        )
    for step in FAR_FIRST:
        begin(remote(block_ref, blocks_out.at[me], 2, step, {"segment": after(step)}))
    begin(remote(own_frame, frames_out.at[core, me], 1, 0, other))
    local_frame.start()
    local_block.start()
    for step in NEAR_FIRST:
        source = after(8 - step)
        slot = frames_out.at[core, source]
        remote(slot, slot, 0, step, {"segment": source}).wait_recv()
        begin(remote(slot, slot, 1, step, other))
    local_frame.wait()
    local_block.wait()
    for step in range(8):
        source = after(8 - step)
        slot = frames_out.at[1 - core, source]
        remote(slot, slot, 1, step, other).wait_recv()
        if step:
            slot = blocks_out.at[source]
            remote(slot, slot, 2, step, {"segment": source}).wait_recv()
    for copy in sends:
        copy.wait_send()


FAR_FIRST = (4, 6, 2, 5, 3, 7, 1)
NEAR_FIRST = (1, 7, 2, 6, 3, 5, 4)


def move(strain_frames, templates):
    anywhere = pl.BlockSpec(memory_space=pl.ANY)
    vmem = pl.BlockSpec(memory_space=pltpu.VMEM)
    received, blocks = pl.pallas_call(
        move_kernel,
        out_shape=(
            jax.ShapeDtypeStruct((2, 8, 16, 1024), BF16),
            jax.ShapeDtypeStruct((8, 16, WIDE), BF16),
        ),
        in_specs=[vmem, vmem],
        out_specs=(anywhere, anywhere),
        scratch_shapes=[
            pltpu.VMEM((8, 16, 1024), F32),
            pltpu.VMEM((9, 16, 1024), BF16),
            pltpu.VMEM((16, WIDE), BF16),
            pltpu.SemaphoreType.DMA((2,)),
            pltpu.SemaphoreType.DMA((3, 8)),
            pltpu.SemaphoreType.DMA((3, 8)),
        ],
        compiler_params=pltpu.CompilerParams(collective_id=0, has_side_effects=True),
    )(strain_frames, templates)
    return received.reshape(256, 1024), blocks.reshape(2 * RADIX_A, WIDE)


def local(strain_frames, frame_slot, templates, bin_edges):
    direct = lax.axis_size("segment") == 8 and strain_frames.shape[1] == 16384
    if direct:
        segment, template = move(strain_frames, templates)
    else:
        segment, template = move_general(strain_frames, frame_slot, templates)
    snr, chisq, peak = compute(bin_edges, frame_slot, segment, template, not direct)
    return (snr.reshape(1, 1, KEPT), chisq.reshape(1, 1, KEPT), peak)


def solution(mesh):
    in_specs = (
        P("segment", None),
        P(),
        P(("groups", "template"), None, "segment"),
        P(("groups", "template"), None),
    )
    out_specs = (
        P("segment", ("groups", "template"), None),
        P("segment", ("groups", "template"), None),
        P("segment", ("groups", "template")),
    )
    return jax.shard_map(local, mesh=mesh, in_specs=in_specs, out_specs=out_specs, check_vma=False)
```

```python
import functools
import functools
import math

import jax
import jax.numpy as jnp
import numpy as np
from jax import lax
from jax.experimental import pallas as pl
from jax.experimental.pallas import tpu as pltpu
from jax.sharding import PartitionSpec as P

RADIX_A = 64
RADIX_B = 32
RADIX_C = 128
LENGTH = RADIX_A * RADIX_B * RADIX_C
INNER = RADIX_B * RADIX_C
KEPT = LENGTH // 2
SUBROWS = 4
WIDE = INNER // 2
F32 = jnp.float32
BF16 = jnp.bfloat16


def dft_table(length, orient):
    counter = np.arange(length)
    angles = orient * 2.0 * math.pi / length * (counter[:, None] * counter[None, :] % length)
    cosine, sine = np.cos(angles), np.sin(angles)
    upper = np.stack([cosine, -sine], axis=1)
    lower = np.stack([sine, cosine], axis=1)
    return np.stack([upper, lower], axis=0).astype(np.float32)


def tables():
    base = dft_table(RADIX_A, -1.0)[:, :, 0, :]
    first_fwd = np.zeros((SUBROWS, 2, RADIX_A, RADIX_A, SUBROWS), np.float32)
    for sub in range(SUBROWS):
        first_fwd[sub, :, :, :, sub] = base
    first_fwd = first_fwd.reshape(SUBROWS * 2 * RADIX_A, RADIX_A * SUBROWS)
    base = dft_table(RADIX_A, 1.0)[:, :, :, : RADIX_A // 2]
    first_inv = np.zeros((2, 2, RADIX_A, 2, RADIX_A // 2, 2), np.float32)
    for half in range(2):
        first_inv[half, :, :, :, :, half] = base
    first_inv = first_inv.reshape(4 * RADIX_A, 2 * RADIX_A)
    third_fwd = dft_table(RADIX_C, -1.0)[:, : RADIX_C // 2].reshape(RADIX_C, 2 * RADIX_C)
    low = RADIX_C // 4
    third_inv = dft_table(RADIX_C, 1.0)[:, low : low + RADIX_C // 2].reshape(RADIX_C, 2 * RADIX_C)
    third_inv = third_inv.astype(BF16).astype(np.float32) / LENGTH
    k1 = np.arange(RADIX_A)[None, :, None]
    q1 = np.arange(RADIX_B)[:, None, None]
    q2 = np.arange(RADIX_C)[None, None, :]
    angle = 2.0 * math.pi / LENGTH * (k1 * (RADIX_C * q1 + q2) % LENGTH)
    turn_one = np.stack([np.cos(angle), np.sin(angle)]).astype(np.float32)
    angle = 2.0 * math.pi / INNER * (q1 * q2 % INNER)
    turn_two = np.stack([np.cos(angle), np.sin(angle)]).astype(np.float32)
    turn_two = np.broadcast_to(turn_two, (2, RADIX_B, 8, RADIX_C)).copy()
    return (
        first_fwd.astype(BF16),
        first_inv.astype(BF16),
        third_fwd.astype(BF16),
        third_inv.astype(BF16),
        turn_one,
        turn_two,
    )


def cadd(a, b):
    return (a[0] + b[0], a[1] + b[1])


def csub(a, b):
    return (a[0] - b[0], a[1] - b[1])


def quarter(a, orient):
    return (-a[1], a[0]) if orient > 0 else (a[1], -a[0])


def spin(a, eighths, orient):
    eighths = eighths % 32
    if eighths == 0:
        return a
    if eighths == 8:
        return quarter(a, orient)
    if eighths == 4:
        root = math.sqrt(0.5)
        b = quarter(a, orient)
        return ((a[0] + b[0]) * root, (a[1] + b[1]) * root)
    angle = orient * 2.0 * math.pi * eighths / 32
    cosine, sine = math.cos(angle), math.sin(angle)
    return (a[0] * cosine - a[1] * sine, a[0] * sine + a[1] * cosine)


def dft4(x, orient):
    a, b = cadd(x[0], x[2]), csub(x[0], x[2])
    c, d = cadd(x[1], x[3]), quarter(csub(x[1], x[3]), orient)
    return [cadd(a, c), cadd(b, d), csub(a, c), csub(b, d)]


def dft8(x, orient):
    even = dft4(x[0::2], orient)
    odd = dft4(x[1::2], orient)
    odd = [spin(v, 4 * k, orient) for k, v in enumerate(odd)]
    return [cadd(e, o) for e, o in zip(even, odd)] + [csub(e, o) for e, o in zip(even, odd)]


def middle(level_ref, per_row, orient, turn_one_ref, turn_two_ref, turned_ref):
    def turn(value, cosine, sine):
        if orient < 0:
            return (value[0] * cosine + value[1] * sine, value[1] * cosine - value[0] * sine)
        return (value[0] * cosine - value[1] * sine, value[0] * sine + value[1] * cosine)

    def group(g, carry):
        start = pl.multiple_of(g * 8, 8)
        rows = pl.ds(start, 8)

        def load(q1):
            block, lane = q1 // per_row, (q1 % per_row) * RADIX_C
            lanes = slice(lane, lane + RADIX_C)
            real = level_ref[pl.ds(pl.multiple_of(block * 2 * RADIX_A + start, 8), 8), lanes]
            imag = level_ref[
                pl.ds(pl.multiple_of((block * 2 + 1) * RADIX_A + start, 8), 8), lanes
            ]
            return turn((real, imag), turn_one_ref[0, q1, rows, :], turn_one_ref[1, q1, rows, :])

        first = []
        for b in range(8):
            four = dft4([load(8 * a + b) for a in range(4)], orient)
            first.append([spin(v, b * ja, orient) for ja, v in enumerate(four)])
        for ja in range(4):
            eight = dft8([first[b][ja] for b in range(8)], orient)
            for jb in range(8):
                j1 = ja + 4 * jb
                value = turn(eight[jb], turn_two_ref[0, j1], turn_two_ref[1, j1])
                out = pl.ds(pl.multiple_of(j1 * RADIX_A + start, 8), 8)
                turned_ref[out, :RADIX_C] = value[0]
                turned_ref[out, RADIX_C:] = value[1]
        return carry

    lax.fori_loop(0, RADIX_A // 8, group, 0)


def last(table_ref, turned_ref, store):
    step = 512
    for chunk in range(WIDE // step):
        block = turned_ref[chunk * step : (chunk + 1) * step, :].astype(BF16)
        store(
            slice(chunk * step, (chunk + 1) * step),
            lax.dot_general(
                table_ref[...], block, (((1,), (1,)), ((), ())), preferred_element_type=F32
            ),
        )


def compute_kernel(edges_ref, slot_ref, *refs, in_order):
    sources, refs = refs[:8], refs[8:]
    snr_ref, chisq_ref, peak_ref = refs[:3]
    level_fwd_ref, level_inv_ref, turned_ref, corr_ref, piece_ref, segment_ref = refs[3:9]
    places, fetch_sem = refs[9:17], refs[17]
    fetches = [
        pltpu.make_async_copy(source, place, fetch_sem.at[number])
        for number, (source, place) in enumerate(zip(sources, places))
    ]
    for number in (0, 2, 6, 7, 4, 1, 3, 5):
        fetches[number].start()
    received_ref, template_ref, first_fwd_ref, first_inv_ref = places[:4]
    third_fwd_ref, third_inv_ref, turn_one_ref, turn_two_ref = places[4:]
    fetches[0].wait()
    if in_order:
        segment_ref = received_ref
    else:
        position = lax.axis_index("segment")
        for kind in range(2):
            half = jnp.minimum(position + kind, 7)
            for source in range(8):
                place = pl.multiple_of((kind * 8 + slot_ref[source, half]) * 16, 16)
                begin = (kind * 8 + source) * 16
                segment_ref[pl.ds(place, 16), :] = received_ref[begin : begin + 16, :]
    fetches[2].wait()
    level_fwd_ref[...] = jnp.dot(
        first_fwd_ref[...], segment_ref[...], preferred_element_type=F32
    )
    fetches[6].wait()
    fetches[7].wait()
    middle(level_fwd_ref, 8, -1, turn_one_ref, turn_two_ref, turned_ref)

    def keep_spectrum(lanes, value):
        corr_ref[:, lanes] = value

    fetches[4].wait()
    last(third_fwd_ref, turned_ref, keep_spectrum)
    for number in (1, 3, 5):
        fetches[number].wait()
    edges = [edges_ref[0, e] for e in range(3)]
    column = lax.broadcasted_iota(jnp.int32, (8, WIDE), 1)
    row = lax.broadcasted_iota(jnp.int32, (8, WIDE), 0)

    def correlate(s, sums):
        place = pl.multiple_of(s * 8, 8)
        both = template_ref[pl.ds(pl.multiple_of(s * 16, 16), 16), :].astype(F32)
        temp_real, temp_imag = both[:8], both[8:]
        upper = pl.ds(place, 8)
        lower = pl.ds(pl.multiple_of(RADIX_A + place, 8), 8)
        spec_real, spec_imag = corr_ref[upper, :], corr_ref[lower, :]
        corr_ref[upper, :] = spec_real * temp_real + spec_imag * temp_imag
        corr_ref[lower, :] = spec_imag * temp_real - spec_real * temp_imag
        power = temp_real * temp_real + temp_imag * temp_imag
        bins = (row + place) * WIDE + column

        def fold(values):
            return jnp.sum(values.reshape(8, WIDE // RADIX_C, RADIX_C), axis=1)

        above = [fold(jnp.where(bins >= edge, power, 0.0)) for edge in edges]
        parts = [fold(power)] + above
        return tuple(a + b for a, b in zip(sums, parts))

    zero = jnp.zeros((8, RADIX_C), F32)
    sums = lax.fori_loop(0, 8, correlate, (zero,) * 4)
    sums = [jnp.sum(v, axis=(0, 1), keepdims=True) for v in sums]
    total = sums[0]
    shares = [
        (sums[0] - sums[1]) / total,
        (sums[1] - sums[2]) / total,
        (sums[2] - sums[3]) / total,
        sums[3] / total,
    ]
    scale = float(LENGTH) / total

    def one_piece(number, carry):
        low = jnp.where(
            number == 0,
            0,
            jnp.where(number == 1, edges[0], jnp.where(number == 2, edges[1], edges[2])),
        )
        high = jnp.where(
            number == 0,
            edges[0],
            jnp.where(number == 1, edges[1], jnp.where(number == 2, edges[2], KEPT)),
        )
        step = 512
        for chunk in range(WIDE // step):
            lanes = slice(chunk * step, (chunk + 1) * step)
            shape = (2, RADIX_A, step)
            bins = (
                lax.broadcasted_iota(jnp.int32, shape, 1) * WIDE
                + lax.broadcasted_iota(jnp.int32, shape, 2)
                + chunk * step
            ).reshape(2 * RADIX_A, step)
            masked = jnp.where((bins >= low) & (bins < high), corr_ref[:, lanes], 0.0)
            level_inv_ref[:, lanes] = jnp.dot(
                first_inv_ref[...], masked.astype(BF16), preferred_element_type=F32
            )
        middle(level_inv_ref, 16, 1, turn_one_ref, turn_two_ref, turned_ref)

        def keep_piece(lanes, value):
            piece_ref[number, :, lanes] = value

        last(third_inv_ref, turned_ref, keep_piece)
        return carry

    lax.fori_loop(0, 4, one_piece, 0)

    def finish(t, best):
        rows = pl.ds(pl.multiple_of(t * 16, 16), 16)
        lower = pl.ds(pl.multiple_of(RADIX_A + t * 16, 16), 16)
        for chunk in range(WIDE // 512):
            lanes = slice(chunk * 512, (chunk + 1) * 512)
            real = [piece_ref[b, rows, lanes] for b in range(4)]
            imag = [piece_ref[b, lower, lanes] for b in range(4)]
            sum_real = real[0] + real[1] + real[2] + real[3]
            sum_imag = imag[0] + imag[1] + imag[2] + imag[3]
            snr = jnp.sqrt((sum_real * sum_real + sum_imag * sum_imag) * scale)
            chisq = jnp.zeros_like(snr)
            for b in range(4):
                diff_real = real[b] - shares[b] * sum_real
                diff_imag = imag[b] - shares[b] * sum_imag
                chisq = chisq + diff_real * diff_real + diff_imag * diff_imag
            chisq = chisq * scale
            reduced = chisq * (1.0 / 6.0)
            base = (1.0 + reduced * reduced * reduced) * 0.5
            weighted = snr * jnp.exp(jnp.log(base) * (-1.0 / 6.0))
            newsnr = jnp.where(reduced > 1.0, weighted, snr)
            snr_ref[rows, lanes] = snr.astype(BF16)
            chisq_ref[rows, lanes] = chisq.astype(BF16)
            for part in range(4):
                best = jnp.maximum(best, newsnr[:, part * RADIX_C : (part + 1) * RADIX_C])
        return best

    best = lax.fori_loop(0, 4, finish, jnp.zeros((16, RADIX_C), F32))
    peak_ref[...] = jnp.max(best, axis=(0, 1), keepdims=True)


def compute(edges, slots, segment, template, in_order):
    vmem = pl.BlockSpec(memory_space=pltpu.VMEM)
    smem = pl.BlockSpec(memory_space=pltpu.SMEM)
    operands = [segment, template] + [jnp.asarray(t) for t in tables()]
    return pl.pallas_call(
        functools.partial(compute_kernel, in_order=in_order),
        out_shape=(
            jax.ShapeDtypeStruct((RADIX_A, WIDE), BF16),
            jax.ShapeDtypeStruct((RADIX_A, WIDE), BF16),
            jax.ShapeDtypeStruct((1, 1), F32),
        ),
        in_specs=[smem] * 2 + [pl.BlockSpec(memory_space=pltpu.HBM)] * 8,
        out_specs=(vmem, vmem, vmem),
        scratch_shapes=[
            pltpu.VMEM((SUBROWS * 2 * RADIX_A, INNER // SUBROWS), F32),
            pltpu.VMEM((4 * RADIX_A, WIDE), F32),
            pltpu.VMEM((WIDE, 2 * RADIX_C), F32),
            pltpu.VMEM((2 * RADIX_A, WIDE), F32),
            pltpu.VMEM((4, 2 * RADIX_A, WIDE), F32),
            pltpu.VMEM((RADIX_A * SUBROWS, INNER // SUBROWS), BF16),
        ]
        + [pltpu.VMEM(operand.shape, operand.dtype) for operand in operands]
        + [pltpu.SemaphoreType.DMA((8,))],
        compiler_params=pltpu.CompilerParams(vmem_limit_bytes=62 * 1024 * 1024),
    )(edges, slots, *operands)


def move_general(strain_frames, frame_slot, templates):
    segments_count = lax.axis_size("segment")
    position = lax.axis_index("segment")
    frame_length = strain_frames.shape[1]
    counter = jnp.arange(segments_count, dtype=jnp.int32)
    slot_now = lax.dynamic_slice_in_dim(frame_slot, position, 1, 1)[:, 0]
    next_index = jnp.minimum(position + 1, segments_count - 1)
    slot_next = lax.dynamic_slice_in_dim(frame_slot, next_index, 1, 1)[:, 0]

    def arrange(slots, frames):
        selector = (counter[:, None] == slots[None, :]).astype(BF16)
        return jnp.dot(selector, frames, preferred_element_type=F32).astype(BF16).reshape(KEPT)

    following_rows = jnp.concatenate(
        [strain_frames[1:], jnp.zeros((1, frame_length), BF16)], axis=0
    )
    outgoing = jnp.stack([strain_frames, following_rows], axis=1)
    received = lax.all_to_all(outgoing, "segment", split_axis=0, concat_axis=0, tiled=True)
    leading = arrange(slot_now, received[:, 0])
    trailing = arrange(slot_next, received[:, 1])
    segment = jnp.concatenate([leading, trailing]).reshape(RADIX_A * SUBROWS, INNER // SUBROWS)
    whole = lax.all_gather(templates, "segment", axis=2, tiled=True)
    template = whole.reshape(2, 8, 8, WIDE).transpose(1, 0, 2, 3).reshape(2 * RADIX_A, WIDE)
    return segment, template


def move_kernel(
    strain_ref,
    template_ref,
    frames_out,
    blocks_out,
    wide_ref,
    frames_ref,
    block_ref,
    local_sem,
    send,
    recv,
):
    me = lax.axis_index("segment")
    core = lax.axis_index("template")
    other = {"template": 1 - core}
    neighbour = me + 1 - 2 * (me % 2)
    beside = {"segment": neighbour}

    def after(step):
        return (me + step) % 8

    barrier = pltpu.get_barrier_semaphore()
    for step in range(1, 8):
        pl.semaphore_signal(
            barrier, inc=1, device_id={"segment": after(step)}, device_id_type=pl.DeviceIdType.MESH
        )
    pl.semaphore_signal(barrier, inc=1, device_id=other, device_id_type=pl.DeviceIdType.MESH)
    parts = [template_ref[0, :, row * WIDE : (row + 1) * WIDE].astype(F32) for row in range(8)]
    rows = [p[c : c + 1] for c in range(2) for p in parts]
    block_ref[...] = jnp.concatenate(rows, axis=0).astype(BF16)
    for row in range(16):
        wide_ref[:, row, :] = strain_ref[:, row * 1024 : (row + 1) * 1024].astype(F32)
    for frame in range(8):
        frames_ref[frame] = wide_ref[frame].astype(BF16)
    frames_ref[8] = jnp.zeros((16, 1024), BF16)
    pl.semaphore_wait(barrier, 8)

    def remote(source, target, row, step, device):
        return pltpu.make_async_remote_copy(
            src_ref=source,
            dst_ref=target,
            send_sem=send.at[row, step],
            recv_sem=recv.at[row, step],
            device_id=device,
            device_id_type=pl.DeviceIdType.MESH,
        )

    own_frame = frames_ref.at[me + core]
    local_frame = pltpu.make_async_copy(own_frame, frames_out.at[core, me], local_sem.at[0])
    local_block = pltpu.make_async_copy(block_ref, blocks_out.at[me], local_sem.at[1])
    sends = []

    def begin(copy):
        copy.start()
        sends.append(copy)

    for step in (4, 6, 2):
        begin(remote(block_ref, blocks_out.at[me], 2, step, {"segment": after(step)}))
    begin(remote(block_ref, blocks_out.at[me], 3, 0, beside))
    for step in FAR_FIRST:
        there = after(step)
        begin(
            remote(
                frames_ref.at[there + core],
                frames_out.at[core, me],
                0,
                step,
                {"segment": there},
            )
        )
    begin(remote(own_frame, frames_out.at[core, me], 1, 0, other))
    local_frame.start()
    local_block.start()
    for step in (2, 6, 4):
        source = after(8 - step)
        slot = blocks_out.at[source]
        remote(slot, slot, 2, step, {"segment": source}).wait_recv()
        begin(remote(slot, slot, 3, step, beside))
    for step in NEAR_FIRST:
        source = after(8 - step)
        slot = frames_out.at[core, source]
        remote(slot, slot, 0, step, {"segment": source}).wait_recv()
        begin(remote(slot, slot, 1, step, other))
    local_frame.wait()
    local_block.wait()
    for step in range(8):
        slot = frames_out.at[1 - core, after(8 - step)]
        remote(slot, slot, 1, step, other).wait_recv()
        if step % 2 == 0:
            slot = blocks_out.at[(neighbour + 8 - step) % 8]
            remote(slot, slot, 3, step, beside).wait_recv()
    for copy in sends:
        copy.wait_send()


FAR_FIRST = (4, 6, 2, 5, 3, 7, 1)
NEAR_FIRST = (1, 7, 2, 6, 3, 5, 4)


def move(strain_frames, templates):
    anywhere = pl.BlockSpec(memory_space=pl.ANY)
    vmem = pl.BlockSpec(memory_space=pltpu.VMEM)
    received, blocks = pl.pallas_call(
        move_kernel,
        out_shape=(
            jax.ShapeDtypeStruct((2, 8, 16, 1024), BF16),
            jax.ShapeDtypeStruct((8, 16, WIDE), BF16),
        ),
        in_specs=[vmem, vmem],
        out_specs=(anywhere, anywhere),
        scratch_shapes=[
            pltpu.VMEM((8, 16, 1024), F32),
            pltpu.VMEM((9, 16, 1024), BF16),
            pltpu.VMEM((16, WIDE), BF16),
            pltpu.SemaphoreType.DMA((2,)),
            pltpu.SemaphoreType.DMA((4, 8)),
            pltpu.SemaphoreType.DMA((4, 8)),
        ],
        compiler_params=pltpu.CompilerParams(collective_id=0, has_side_effects=True),
    )(strain_frames, templates)
    return received.reshape(256, 1024), blocks.reshape(2 * RADIX_A, WIDE)


def local(strain_frames, frame_slot, templates, bin_edges):
    direct = lax.axis_size("segment") == 8 and strain_frames.shape[1] == 16384
    if direct:
        segment, template = move(strain_frames, templates)
    else:
        segment, template = move_general(strain_frames, frame_slot, templates)
    snr, chisq, peak = compute(bin_edges, frame_slot, segment, template, not direct)
    return (snr.reshape(1, 1, KEPT), chisq.reshape(1, 1, KEPT), peak)


def solution(mesh):
    in_specs = (
        P("segment", None),
        P(),
        P(("groups", "template"), None, "segment"),
        P(("groups", "template"), None),
    )
    out_specs = (
        P("segment", ("groups", "template"), None),
        P("segment", ("groups", "template"), None),
        P("segment", ("groups", "template")),
    )
    return jax.shard_map(local, mesh=mesh, in_specs=in_specs, out_specs=out_specs, check_vma=False)
```

```python
import functools
import functools
import math

import jax
import jax.numpy as jnp
import numpy as np
from jax import lax
from jax.experimental import pallas as pl
from jax.experimental.pallas import tpu as pltpu
from jax.sharding import PartitionSpec as P

RADIX_A = 64
RADIX_B = 32
RADIX_C = 128
LENGTH = RADIX_A * RADIX_B * RADIX_C
INNER = RADIX_B * RADIX_C
KEPT = LENGTH // 2
SUBROWS = 4
WIDE = INNER // 2
F32 = jnp.float32
BF16 = jnp.bfloat16


def dft_table(length, orient):
    counter = np.arange(length)
    angles = orient * 2.0 * math.pi / length * (counter[:, None] * counter[None, :] % length)
    cosine, sine = np.cos(angles), np.sin(angles)
    upper = np.stack([cosine, -sine], axis=1)
    lower = np.stack([sine, cosine], axis=1)
    return np.stack([upper, lower], axis=0).astype(np.float32)


def tables():
    base = dft_table(RADIX_A, -1.0)[:, :, 0, :]
    first_fwd = np.zeros((SUBROWS, 2, RADIX_A, RADIX_A, SUBROWS), np.float32)
    for sub in range(SUBROWS):
        first_fwd[sub, :, :, :, sub] = base
    first_fwd = first_fwd.reshape(SUBROWS * 2 * RADIX_A, RADIX_A * SUBROWS)
    base = dft_table(RADIX_A, 1.0)[:, :, :, : RADIX_A // 2]
    first_inv = np.zeros((2, 2, RADIX_A, 2, RADIX_A // 2, 2), np.float32)
    for half in range(2):
        first_inv[half, :, :, :, :, half] = base
    first_inv = first_inv.reshape(4 * RADIX_A, 2 * RADIX_A)
    third_fwd = dft_table(RADIX_C, -1.0)[:, : RADIX_C // 2].reshape(RADIX_C, 2 * RADIX_C)
    low = RADIX_C // 4
    third_inv = dft_table(RADIX_C, 1.0)[:, low : low + RADIX_C // 2].reshape(RADIX_C, 2 * RADIX_C)
    third_inv = third_inv.astype(BF16).astype(np.float32) / LENGTH
    k1 = np.arange(RADIX_A)[None, :, None]
    q1 = np.arange(RADIX_B)[:, None, None]
    q2 = np.arange(RADIX_C)[None, None, :]
    angle = 2.0 * math.pi / LENGTH * (k1 * (RADIX_C * q1 + q2) % LENGTH)
    turn_one = np.stack([np.cos(angle), np.sin(angle)]).astype(np.float32)
    angle = 2.0 * math.pi / INNER * (q1 * q2 % INNER)
    turn_two = np.stack([np.cos(angle), np.sin(angle)]).astype(np.float32)
    turn_two = np.broadcast_to(turn_two, (2, RADIX_B, 8, RADIX_C)).copy()
    return (
        first_fwd.astype(BF16),
        first_inv.astype(BF16),
        third_fwd.astype(BF16),
        third_inv.astype(BF16),
        turn_one,
        turn_two,
    )


def cadd(a, b):
    return (a[0] + b[0], a[1] + b[1])


def csub(a, b):
    return (a[0] - b[0], a[1] - b[1])


def quarter(a, orient):
    return (-a[1], a[0]) if orient > 0 else (a[1], -a[0])


def spin(a, eighths, orient):
    eighths = eighths % 32
    if eighths == 0:
        return a
    if eighths == 8:
        return quarter(a, orient)
    if eighths == 4:
        root = math.sqrt(0.5)
        b = quarter(a, orient)
        return ((a[0] + b[0]) * root, (a[1] + b[1]) * root)
    angle = orient * 2.0 * math.pi * eighths / 32
    cosine, sine = math.cos(angle), math.sin(angle)
    return (a[0] * cosine - a[1] * sine, a[0] * sine + a[1] * cosine)


def dft4(x, orient):
    a, b = cadd(x[0], x[2]), csub(x[0], x[2])
    c, d = cadd(x[1], x[3]), quarter(csub(x[1], x[3]), orient)
    return [cadd(a, c), cadd(b, d), csub(a, c), csub(b, d)]


def dft8(x, orient):
    even = dft4(x[0::2], orient)
    odd = dft4(x[1::2], orient)
    odd = [spin(v, 4 * k, orient) for k, v in enumerate(odd)]
    return [cadd(e, o) for e, o in zip(even, odd)] + [csub(e, o) for e, o in zip(even, odd)]


def middle(level_ref, per_row, orient, turn_one_ref, turn_two_ref, turned_ref):
    def turn(value, cosine, sine):
        if orient < 0:
            return (value[0] * cosine + value[1] * sine, value[1] * cosine - value[0] * sine)
        return (value[0] * cosine - value[1] * sine, value[0] * sine + value[1] * cosine)

    def group(g, carry):
        start = pl.multiple_of(g * 8, 8)
        rows = pl.ds(start, 8)

        def load(q1):
            block, lane = q1 // per_row, (q1 % per_row) * RADIX_C
            lanes = slice(lane, lane + RADIX_C)
            real = level_ref[pl.ds(pl.multiple_of(block * 2 * RADIX_A + start, 8), 8), lanes]
            imag = level_ref[
                pl.ds(pl.multiple_of((block * 2 + 1) * RADIX_A + start, 8), 8), lanes
            ]
            return turn((real, imag), turn_one_ref[0, q1, rows, :], turn_one_ref[1, q1, rows, :])

        first = []
        for b in range(8):
            four = dft4([load(8 * a + b) for a in range(4)], orient)
            first.append([spin(v, b * ja, orient) for ja, v in enumerate(four)])
        for ja in range(4):
            eight = dft8([first[b][ja] for b in range(8)], orient)
            for jb in range(8):
                j1 = ja + 4 * jb
                value = turn(eight[jb], turn_two_ref[0, j1], turn_two_ref[1, j1])
                out = pl.ds(pl.multiple_of(j1 * RADIX_A + start, 8), 8)
                turned_ref[out, :RADIX_C] = value[0]
                turned_ref[out, RADIX_C:] = value[1]
        return carry

    lax.fori_loop(0, RADIX_A // 8, group, 0)


def last(table_ref, turned_ref, store):
    step = 512
    for chunk in range(WIDE // step):
        block = turned_ref[chunk * step : (chunk + 1) * step, :].astype(BF16)
        store(
            slice(chunk * step, (chunk + 1) * step),
            lax.dot_general(
                table_ref[...], block, (((1,), (1,)), ((), ())), preferred_element_type=F32
            ),
        )


def compute_kernel(edges_ref, slot_ref, *refs, in_order):
    sources, refs = refs[:8], refs[8:]
    snr_ref, chisq_ref, peak_ref = refs[:3]
    level_fwd_ref, level_inv_ref, turned_ref, corr_ref, piece_ref, segment_ref = refs[3:9]
    places, fetch_sem = refs[9:17], refs[17]
    fetches = [
        pltpu.make_async_copy(source, place, fetch_sem.at[number])
        for number, (source, place) in enumerate(zip(sources, places))
    ]
    for number in (0, 2, 6, 7, 4, 1, 3, 5):
        fetches[number].start()
    received_ref, template_ref, first_fwd_ref, first_inv_ref = places[:4]
    third_fwd_ref, third_inv_ref, turn_one_ref, turn_two_ref = places[4:]
    fetches[0].wait()
    if in_order:
        segment_ref = received_ref
    else:
        position = lax.axis_index("segment")
        for kind in range(2):
            half = jnp.minimum(position + kind, 7)
            for source in range(8):
                place = pl.multiple_of((kind * 8 + slot_ref[source, half]) * 16, 16)
                begin = (kind * 8 + source) * 16
                segment_ref[pl.ds(place, 16), :] = received_ref[begin : begin + 16, :]
    fetches[2].wait()
    level_fwd_ref[...] = jnp.dot(
        first_fwd_ref[...], segment_ref[...], preferred_element_type=F32
    )
    fetches[6].wait()
    fetches[7].wait()
    middle(level_fwd_ref, 8, -1, turn_one_ref, turn_two_ref, turned_ref)

    def keep_spectrum(lanes, value):
        corr_ref[:, lanes] = value

    fetches[4].wait()
    last(third_fwd_ref, turned_ref, keep_spectrum)
    for number in (1, 3, 5):
        fetches[number].wait()
    edges = [edges_ref[0, e] for e in range(3)]
    column = lax.broadcasted_iota(jnp.int32, (8, WIDE), 1)
    row = lax.broadcasted_iota(jnp.int32, (8, WIDE), 0)

    def correlate(s, sums):
        place = pl.multiple_of(s * 8, 8)
        both = template_ref[pl.ds(pl.multiple_of(s * 16, 16), 16), :].astype(F32)
        temp_real, temp_imag = both[:8], both[8:]
        upper = pl.ds(place, 8)
        lower = pl.ds(pl.multiple_of(RADIX_A + place, 8), 8)
        spec_real, spec_imag = corr_ref[upper, :], corr_ref[lower, :]
        corr_ref[upper, :] = spec_real * temp_real + spec_imag * temp_imag
        corr_ref[lower, :] = spec_imag * temp_real - spec_real * temp_imag
        power = temp_real * temp_real + temp_imag * temp_imag
        bins = (row + place) * WIDE + column

        def fold(values):
            return jnp.sum(values.reshape(8, WIDE // RADIX_C, RADIX_C), axis=1)

        above = [fold(jnp.where(bins >= edge, power, 0.0)) for edge in edges]
        parts = [fold(power)] + above
        return tuple(a + b for a, b in zip(sums, parts))

    zero = jnp.zeros((8, RADIX_C), F32)
    sums = lax.fori_loop(0, 8, correlate, (zero,) * 4)
    sums = [jnp.sum(v, axis=(0, 1), keepdims=True) for v in sums]
    total = sums[0]
    shares = [
        (sums[0] - sums[1]) / total,
        (sums[1] - sums[2]) / total,
        (sums[2] - sums[3]) / total,
        sums[3] / total,
    ]
    scale = float(LENGTH) / total

    def one_piece(number, carry):
        low = jnp.where(
            number == 0,
            0,
            jnp.where(number == 1, edges[0], jnp.where(number == 2, edges[1], edges[2])),
        )
        high = jnp.where(
            number == 0,
            edges[0],
            jnp.where(number == 1, edges[1], jnp.where(number == 2, edges[2], KEPT)),
        )
        step = 512
        for chunk in range(WIDE // step):
            lanes = slice(chunk * step, (chunk + 1) * step)
            shape = (2, RADIX_A, step)
            bins = (
                lax.broadcasted_iota(jnp.int32, shape, 1) * WIDE
                + lax.broadcasted_iota(jnp.int32, shape, 2)
                + chunk * step
            ).reshape(2 * RADIX_A, step)
            masked = jnp.where((bins >= low) & (bins < high), corr_ref[:, lanes], 0.0)
            level_inv_ref[:, lanes] = jnp.dot(
                first_inv_ref[...], masked.astype(BF16), preferred_element_type=F32
            )
        middle(level_inv_ref, 16, 1, turn_one_ref, turn_two_ref, turned_ref)

        def keep_piece(lanes, value):
            piece_ref[number, :, lanes] = value

        last(third_inv_ref, turned_ref, keep_piece)
        return carry

    lax.fori_loop(0, 4, one_piece, 0)

    def finish(t, best):
        rows = pl.ds(pl.multiple_of(t * 16, 16), 16)
        lower = pl.ds(pl.multiple_of(RADIX_A + t * 16, 16), 16)
        for chunk in range(WIDE // 512):
            lanes = slice(chunk * 512, (chunk + 1) * 512)
            real = [piece_ref[b, rows, lanes] for b in range(4)]
            imag = [piece_ref[b, lower, lanes] for b in range(4)]
            sum_real = real[0] + real[1] + real[2] + real[3]
            sum_imag = imag[0] + imag[1] + imag[2] + imag[3]
            snr = jnp.sqrt((sum_real * sum_real + sum_imag * sum_imag) * scale)
            chisq = jnp.zeros_like(snr)
            for b in range(4):
                diff_real = real[b] - shares[b] * sum_real
                diff_imag = imag[b] - shares[b] * sum_imag
                chisq = chisq + diff_real * diff_real + diff_imag * diff_imag
            chisq = chisq * scale
            reduced = chisq * (1.0 / 6.0)
            base = (1.0 + reduced * reduced * reduced) * 0.5
            weighted = snr * jnp.exp(jnp.log(base) * (-1.0 / 6.0))
            newsnr = jnp.where(reduced > 1.0, weighted, snr)
            for line in range(16):
                begin = pl.multiple_of((t * 16 + line) * WIDE + chunk * 512, 512)
                snr_ref[0, :, pl.ds(begin, 512)] = snr[line : line + 1].astype(BF16)
                chisq_ref[0, :, pl.ds(begin, 512)] = chisq[line : line + 1].astype(BF16)
            for part in range(4):
                best = jnp.maximum(best, newsnr[:, part * RADIX_C : (part + 1) * RADIX_C])
        return best

    best = lax.fori_loop(0, 4, finish, jnp.zeros((16, RADIX_C), F32))
    peak_ref[...] = jnp.max(best, axis=(0, 1), keepdims=True)


def compute(edges, slots, segment, template, in_order):
    vmem = pl.BlockSpec(memory_space=pltpu.VMEM)
    smem = pl.BlockSpec(memory_space=pltpu.SMEM)
    operands = [segment, template] + [jnp.asarray(t) for t in tables()]
    return pl.pallas_call(
        functools.partial(compute_kernel, in_order=in_order),
        out_shape=(
            jax.ShapeDtypeStruct((1, 1, KEPT), BF16),
            jax.ShapeDtypeStruct((1, 1, KEPT), BF16),
            jax.ShapeDtypeStruct((1, 1), F32),
        ),
        in_specs=[smem] * 2 + [pl.BlockSpec(memory_space=pltpu.HBM)] * 8,
        out_specs=(vmem, vmem, vmem),
        scratch_shapes=[
            pltpu.VMEM((SUBROWS * 2 * RADIX_A, INNER // SUBROWS), F32),
            pltpu.VMEM((4 * RADIX_A, WIDE), F32),
            pltpu.VMEM((WIDE, 2 * RADIX_C), F32),
            pltpu.VMEM((2 * RADIX_A, WIDE), F32),
            pltpu.VMEM((4, 2 * RADIX_A, WIDE), F32),
            pltpu.VMEM((RADIX_A * SUBROWS, INNER // SUBROWS), BF16),
        ]
        + [pltpu.VMEM(operand.shape, operand.dtype) for operand in operands]
        + [pltpu.SemaphoreType.DMA((8,))],
        compiler_params=pltpu.CompilerParams(vmem_limit_bytes=62 * 1024 * 1024),
    )(edges, slots, *operands)


def move_general(strain_frames, frame_slot, templates):
    segments_count = lax.axis_size("segment")
    position = lax.axis_index("segment")
    frame_length = strain_frames.shape[1]
    counter = jnp.arange(segments_count, dtype=jnp.int32)
    slot_now = lax.dynamic_slice_in_dim(frame_slot, position, 1, 1)[:, 0]
    next_index = jnp.minimum(position + 1, segments_count - 1)
    slot_next = lax.dynamic_slice_in_dim(frame_slot, next_index, 1, 1)[:, 0]

    def arrange(slots, frames):
        selector = (counter[:, None] == slots[None, :]).astype(BF16)
        return jnp.dot(selector, frames, preferred_element_type=F32).astype(BF16).reshape(KEPT)

    following_rows = jnp.concatenate(
        [strain_frames[1:], jnp.zeros((1, frame_length), BF16)], axis=0
    )
    outgoing = jnp.stack([strain_frames, following_rows], axis=1)
    received = lax.all_to_all(outgoing, "segment", split_axis=0, concat_axis=0, tiled=True)
    leading = arrange(slot_now, received[:, 0])
    trailing = arrange(slot_next, received[:, 1])
    segment = jnp.concatenate([leading, trailing]).reshape(RADIX_A * SUBROWS, INNER // SUBROWS)
    whole = lax.all_gather(templates, "segment", axis=2, tiled=True)
    template = whole.reshape(2, 8, 8, WIDE).transpose(1, 0, 2, 3).reshape(2 * RADIX_A, WIDE)
    return segment, template


def move_kernel(
    strain_ref,
    template_ref,
    frames_out,
    blocks_out,
    wide_ref,
    frames_ref,
    block_ref,
    local_sem,
    send,
    recv,
):
    me = lax.axis_index("segment")
    core = lax.axis_index("template")
    other = {"template": 1 - core}
    neighbour = me + 1 - 2 * (me % 2)
    beside = {"segment": neighbour}

    def after(step):
        return (me + step) % 8

    barrier = pltpu.get_barrier_semaphore()
    for step in range(1, 8):
        pl.semaphore_signal(
            barrier, inc=1, device_id={"segment": after(step)}, device_id_type=pl.DeviceIdType.MESH
        )
    pl.semaphore_signal(barrier, inc=1, device_id=other, device_id_type=pl.DeviceIdType.MESH)
    parts = [template_ref[0, :, row * WIDE : (row + 1) * WIDE].astype(F32) for row in range(8)]
    rows = [p[c : c + 1] for c in range(2) for p in parts]
    block_ref[...] = jnp.concatenate(rows, axis=0).astype(BF16)
    for row in range(16):
        wide_ref[:, row, :] = strain_ref[:, row * 1024 : (row + 1) * 1024].astype(F32)
    for frame in range(8):
        frames_ref[frame] = wide_ref[frame].astype(BF16)
    frames_ref[8] = jnp.zeros((16, 1024), BF16)
    pl.semaphore_wait(barrier, 8)

    def remote(source, target, row, step, device):
        return pltpu.make_async_remote_copy(
            src_ref=source,
            dst_ref=target,
            send_sem=send.at[row, step],
            recv_sem=recv.at[row, step],
            device_id=device,
            device_id_type=pl.DeviceIdType.MESH,
        )

    own_frame = frames_ref.at[me + core]
    local_frame = pltpu.make_async_copy(own_frame, frames_out.at[core, me], local_sem.at[0])
    local_block = pltpu.make_async_copy(block_ref, blocks_out.at[me], local_sem.at[1])
    sends = []

    def begin(copy):
        copy.start()
        sends.append(copy)

    for step in (4, 6, 2):
        begin(remote(block_ref, blocks_out.at[me], 2, step, {"segment": after(step)}))
    begin(remote(block_ref, blocks_out.at[me], 3, 0, beside))
    for step in FAR_FIRST:
        there = after(step)
        begin(
            remote(
                frames_ref.at[there + core],
                frames_out.at[core, me],
                0,
                step,
                {"segment": there},
            )
        )
    begin(remote(own_frame, frames_out.at[core, me], 1, 0, other))
    local_frame.start()
    local_block.start()
    for step in (2, 6, 4):
        source = after(8 - step)
        slot = blocks_out.at[source]
        remote(slot, slot, 2, step, {"segment": source}).wait_recv()
        begin(remote(slot, slot, 3, step, beside))
    for step in NEAR_FIRST:
        source = after(8 - step)
        slot = frames_out.at[core, source]
        remote(slot, slot, 0, step, {"segment": source}).wait_recv()
        begin(remote(slot, slot, 1, step, other))
    local_frame.wait()
    local_block.wait()
    for step in range(8):
        slot = frames_out.at[1 - core, after(8 - step)]
        remote(slot, slot, 1, step, other).wait_recv()
        if step % 2 == 0:
            slot = blocks_out.at[(neighbour + 8 - step) % 8]
            remote(slot, slot, 3, step, beside).wait_recv()
    for copy in sends:
        copy.wait_send()


FAR_FIRST = (4, 6, 2, 5, 3, 7, 1)
NEAR_FIRST = (1, 7, 2, 6, 3, 5, 4)


def move(strain_frames, templates):
    anywhere = pl.BlockSpec(memory_space=pl.ANY)
    vmem = pl.BlockSpec(memory_space=pltpu.VMEM)
    received, blocks = pl.pallas_call(
        move_kernel,
        out_shape=(
            jax.ShapeDtypeStruct((2, 8, 16, 1024), BF16),
            jax.ShapeDtypeStruct((8, 16, WIDE), BF16),
        ),
        in_specs=[vmem, vmem],
        out_specs=(anywhere, anywhere),
        scratch_shapes=[
            pltpu.VMEM((8, 16, 1024), F32),
            pltpu.VMEM((9, 16, 1024), BF16),
            pltpu.VMEM((16, WIDE), BF16),
            pltpu.SemaphoreType.DMA((2,)),
            pltpu.SemaphoreType.DMA((4, 8)),
            pltpu.SemaphoreType.DMA((4, 8)),
        ],
        compiler_params=pltpu.CompilerParams(collective_id=0, has_side_effects=True),
    )(strain_frames, templates)
    return received.reshape(256, 1024), blocks.reshape(2 * RADIX_A, WIDE)


def local(strain_frames, frame_slot, templates, bin_edges):
    direct = lax.axis_size("segment") == 8 and strain_frames.shape[1] == 16384
    if direct:
        segment, template = move(strain_frames, templates)
    else:
        segment, template = move_general(strain_frames, frame_slot, templates)
    snr, chisq, peak = compute(bin_edges, frame_slot, segment, template, not direct)
    return (snr, chisq, peak)


def solution(mesh):
    in_specs = (
        P("segment", None),
        P(),
        P(("groups", "template"), None, "segment"),
        P(("groups", "template"), None),
    )
    out_specs = (
        P("segment", ("groups", "template"), None),
        P("segment", ("groups", "template"), None),
        P("segment", ("groups", "template")),
    )
    return jax.shard_map(local, mesh=mesh, in_specs=in_specs, out_specs=out_specs, check_vma=False)
```

```python
import functools
import functools
import math

import jax
import jax.numpy as jnp
import numpy as np
from jax import lax
from jax.experimental import pallas as pl
from jax.experimental.pallas import tpu as pltpu
from jax.sharding import PartitionSpec as P

RADIX_A = 64
RADIX_B = 32
RADIX_C = 128
LENGTH = RADIX_A * RADIX_B * RADIX_C
INNER = RADIX_B * RADIX_C
KEPT = LENGTH // 2
SUBROWS = 4
WIDE = INNER // 2
F32 = jnp.float32
BF16 = jnp.bfloat16


def dft_table(length, orient):
    counter = np.arange(length)
    angles = orient * 2.0 * math.pi / length * (counter[:, None] * counter[None, :] % length)
    cosine, sine = np.cos(angles), np.sin(angles)
    upper = np.stack([cosine, -sine], axis=1)
    lower = np.stack([sine, cosine], axis=1)
    return np.stack([upper, lower], axis=0).astype(np.float32)


def tables():
    base = dft_table(RADIX_A, -1.0)[:, :, 0, :]
    first_fwd = np.zeros((SUBROWS, 2, RADIX_A, RADIX_A, SUBROWS), np.float32)
    for sub in range(SUBROWS):
        first_fwd[sub, :, :, :, sub] = base
    first_fwd = first_fwd.reshape(SUBROWS * 2 * RADIX_A, RADIX_A * SUBROWS)
    base = dft_table(RADIX_A, 1.0)[:, :, :, : RADIX_A // 2]
    first_inv = np.zeros((2, 2, RADIX_A, 2, RADIX_A // 2, 2), np.float32)
    for half in range(2):
        first_inv[half, :, :, :, :, half] = base
    first_inv = first_inv.reshape(4 * RADIX_A, 2 * RADIX_A)
    third_fwd = dft_table(RADIX_C, -1.0)[:, : RADIX_C // 2].reshape(RADIX_C, 2 * RADIX_C)
    low = RADIX_C // 4
    third_inv = dft_table(RADIX_C, 1.0)[:, low : low + RADIX_C // 2].reshape(RADIX_C, 2 * RADIX_C)
    third_inv = third_inv.astype(BF16).astype(np.float32) / LENGTH
    k1 = np.arange(RADIX_A)[None, :, None]
    q1 = np.arange(RADIX_B)[:, None, None]
    q2 = np.arange(RADIX_C)[None, None, :]
    angle = 2.0 * math.pi / LENGTH * (k1 * (RADIX_C * q1 + q2) % LENGTH)
    turn_one = np.stack([np.cos(angle), np.sin(angle)]).astype(np.float32)
    angle = 2.0 * math.pi / INNER * (q1 * q2 % INNER)
    turn_two = np.stack([np.cos(angle), np.sin(angle)]).astype(np.float32)
    turn_two = np.broadcast_to(turn_two, (2, RADIX_B, 8, RADIX_C)).copy()
    return (
        first_fwd.astype(BF16),
        first_inv.astype(BF16),
        third_fwd.astype(BF16),
        third_inv.astype(BF16),
        turn_one,
        turn_two,
    )


def cadd(a, b):
    return (a[0] + b[0], a[1] + b[1])


def csub(a, b):
    return (a[0] - b[0], a[1] - b[1])


def quarter(a, orient):
    return (-a[1], a[0]) if orient > 0 else (a[1], -a[0])


def spin(a, eighths, orient):
    eighths = eighths % 32
    if eighths == 0:
        return a
    if eighths == 8:
        return quarter(a, orient)
    if eighths == 4:
        root = math.sqrt(0.5)
        b = quarter(a, orient)
        return ((a[0] + b[0]) * root, (a[1] + b[1]) * root)
    angle = orient * 2.0 * math.pi * eighths / 32
    cosine, sine = math.cos(angle), math.sin(angle)
    return (a[0] * cosine - a[1] * sine, a[0] * sine + a[1] * cosine)


def dft4(x, orient):
    a, b = cadd(x[0], x[2]), csub(x[0], x[2])
    c, d = cadd(x[1], x[3]), quarter(csub(x[1], x[3]), orient)
    return [cadd(a, c), cadd(b, d), csub(a, c), csub(b, d)]


def dft8(x, orient):
    even = dft4(x[0::2], orient)
    odd = dft4(x[1::2], orient)
    odd = [spin(v, 4 * k, orient) for k, v in enumerate(odd)]
    return [cadd(e, o) for e, o in zip(even, odd)] + [csub(e, o) for e, o in zip(even, odd)]


def middle(level_ref, per_row, orient, turn_one_ref, turn_two_ref, turned_ref):
    def turn(value, cosine, sine):
        if orient < 0:
            return (value[0] * cosine + value[1] * sine, value[1] * cosine - value[0] * sine)
        return (value[0] * cosine - value[1] * sine, value[0] * sine + value[1] * cosine)

    def group(g, carry):
        start = pl.multiple_of(g * 8, 8)
        rows = pl.ds(start, 8)

        def load(q1):
            block, lane = q1 // per_row, (q1 % per_row) * RADIX_C
            lanes = slice(lane, lane + RADIX_C)
            real = level_ref[pl.ds(pl.multiple_of(block * 2 * RADIX_A + start, 8), 8), lanes]
            imag = level_ref[
                pl.ds(pl.multiple_of((block * 2 + 1) * RADIX_A + start, 8), 8), lanes
            ]
            return turn((real, imag), turn_one_ref[0, q1, rows, :], turn_one_ref[1, q1, rows, :])

        first = []
        for b in range(8):
            four = dft4([load(8 * a + b) for a in range(4)], orient)
            first.append([spin(v, b * ja, orient) for ja, v in enumerate(four)])
        for ja in range(4):
            eight = dft8([first[b][ja] for b in range(8)], orient)
            for jb in range(8):
                j1 = ja + 4 * jb
                value = turn(eight[jb], turn_two_ref[0, j1], turn_two_ref[1, j1])
                out = pl.ds(pl.multiple_of(j1 * RADIX_A + start, 8), 8)
                turned_ref[out, :RADIX_C] = value[0]
                turned_ref[out, RADIX_C:] = value[1]
        return carry

    lax.fori_loop(0, RADIX_A // 8, group, 0)


def last(table_ref, turned_ref, store):
    step = 512
    for chunk in range(WIDE // step):
        block = turned_ref[chunk * step : (chunk + 1) * step, :].astype(BF16)
        store(
            slice(chunk * step, (chunk + 1) * step),
            lax.dot_general(
                table_ref[...], block, (((1,), (1,)), ((), ())), preferred_element_type=F32
            ),
        )


def compute_kernel(edges_ref, slot_ref, *refs, in_order):
    sources, refs = refs[:8], refs[8:]
    snr_ref, chisq_ref, peak_ref = refs[:3]
    level_fwd_ref, level_inv_ref, turned_ref, corr_ref, piece_ref, segment_ref = refs[3:9]
    places, fetch_sem = refs[9:17], refs[17]
    fetches = [
        pltpu.make_async_copy(source, place, fetch_sem.at[number])
        for number, (source, place) in enumerate(zip(sources, places))
    ]
    for number in (0, 2, 6, 7, 4, 1, 3, 5):
        fetches[number].start()
    received_ref, template_ref, first_fwd_ref, first_inv_ref = places[:4]
    third_fwd_ref, third_inv_ref, turn_one_ref, turn_two_ref = places[4:]
    fetches[0].wait()
    if in_order:
        segment_ref = received_ref
    else:
        position = lax.axis_index("segment")
        for kind in range(2):
            half = jnp.minimum(position + kind, 7)
            for source in range(8):
                place = pl.multiple_of((kind * 8 + slot_ref[source, half]) * 16, 16)
                begin = (kind * 8 + source) * 16
                segment_ref[pl.ds(place, 16), :] = received_ref[begin : begin + 16, :]
    fetches[2].wait()
    level_fwd_ref[...] = jnp.dot(
        first_fwd_ref[...], segment_ref[...], preferred_element_type=F32
    )
    fetches[6].wait()
    fetches[7].wait()
    middle(level_fwd_ref, 8, -1, turn_one_ref, turn_two_ref, turned_ref)

    def keep_spectrum(lanes, value):
        corr_ref[:, lanes] = value

    fetches[4].wait()
    last(third_fwd_ref, turned_ref, keep_spectrum)
    for number in (1, 3, 5):
        fetches[number].wait()
    edges = [edges_ref[0, e] for e in range(3)]
    column = lax.broadcasted_iota(jnp.int32, (8, WIDE), 1)
    row = lax.broadcasted_iota(jnp.int32, (8, WIDE), 0)

    def correlate(s, sums):
        place = pl.multiple_of(s * 8, 8)
        both = template_ref[pl.ds(pl.multiple_of(s * 16, 16), 16), :].astype(F32)
        temp_real, temp_imag = both[:8], both[8:]
        upper = pl.ds(place, 8)
        lower = pl.ds(pl.multiple_of(RADIX_A + place, 8), 8)
        spec_real, spec_imag = corr_ref[upper, :], corr_ref[lower, :]
        corr_ref[upper, :] = spec_real * temp_real + spec_imag * temp_imag
        corr_ref[lower, :] = spec_imag * temp_real - spec_real * temp_imag
        power = temp_real * temp_real + temp_imag * temp_imag
        bins = (row + place) * WIDE + column

        def fold(values):
            return jnp.sum(values.reshape(8, WIDE // RADIX_C, RADIX_C), axis=1)

        above = [fold(jnp.where(bins >= edge, power, 0.0)) for edge in edges]
        parts = [fold(power)] + above
        return tuple(a + b for a, b in zip(sums, parts))

    zero = jnp.zeros((8, RADIX_C), F32)
    sums = lax.fori_loop(0, 8, correlate, (zero,) * 4)
    sums = [jnp.sum(v, axis=(0, 1), keepdims=True) for v in sums]
    total = sums[0]
    shares = [
        (sums[0] - sums[1]) / total,
        (sums[1] - sums[2]) / total,
        (sums[2] - sums[3]) / total,
        sums[3] / total,
    ]
    scale = float(LENGTH) / total

    def one_piece(number, carry):
        low = jnp.where(
            number == 0,
            0,
            jnp.where(number == 1, edges[0], jnp.where(number == 2, edges[1], edges[2])),
        )
        high = jnp.where(
            number == 0,
            edges[0],
            jnp.where(number == 1, edges[1], jnp.where(number == 2, edges[2], KEPT)),
        )
        step = 512
        for chunk in range(WIDE // step):
            lanes = slice(chunk * step, (chunk + 1) * step)
            shape = (2, RADIX_A, step)
            bins = (
                lax.broadcasted_iota(jnp.int32, shape, 1) * WIDE
                + lax.broadcasted_iota(jnp.int32, shape, 2)
                + chunk * step
            ).reshape(2 * RADIX_A, step)
            masked = jnp.where((bins >= low) & (bins < high), corr_ref[:, lanes], 0.0)
            level_inv_ref[:, lanes] = jnp.dot(
                first_inv_ref[...], masked.astype(BF16), preferred_element_type=F32
            )
        middle(level_inv_ref, 16, 1, turn_one_ref, turn_two_ref, turned_ref)

        def keep_piece(lanes, value):
            piece_ref[number, :, lanes] = value

        last(third_inv_ref, turned_ref, keep_piece)
        return carry

    lax.fori_loop(0, 4, one_piece, 0)

    def finish(t, best):
        rows = pl.ds(pl.multiple_of(t * 16, 16), 16)
        lower = pl.ds(pl.multiple_of(RADIX_A + t * 16, 16), 16)
        for chunk in range(WIDE // 512):
            lanes = slice(chunk * 512, (chunk + 1) * 512)
            real = [piece_ref[b, rows, lanes] for b in range(4)]
            imag = [piece_ref[b, lower, lanes] for b in range(4)]
            sum_real = real[0] + real[1] + real[2] + real[3]
            sum_imag = imag[0] + imag[1] + imag[2] + imag[3]
            snr = jnp.sqrt((sum_real * sum_real + sum_imag * sum_imag) * scale)
            chisq = jnp.zeros_like(snr)
            for b in range(4):
                diff_real = real[b] - shares[b] * sum_real
                diff_imag = imag[b] - shares[b] * sum_imag
                chisq = chisq + diff_real * diff_real + diff_imag * diff_imag
            chisq = chisq * scale
            reduced = chisq * (1.0 / 6.0)
            base = (1.0 + reduced * reduced * reduced) * 0.5
            weighted = snr * jnp.exp(jnp.log(base) * (-1.0 / 6.0))
            newsnr = jnp.where(reduced > 1.0, weighted, snr)
            for line in range(16):
                begin = pl.multiple_of((t * 16 + line) * WIDE + chunk * 512, 512)
                snr_ref[0, :, pl.ds(begin, 512)] = snr[line : line + 1].astype(BF16)
                chisq_ref[0, :, pl.ds(begin, 512)] = chisq[line : line + 1].astype(BF16)
            for part in range(4):
                best = jnp.maximum(best, newsnr[:, part * RADIX_C : (part + 1) * RADIX_C])
        return best

    best = lax.fori_loop(0, 4, finish, jnp.zeros((16, RADIX_C), F32))
    peak_ref[...] = jnp.max(best, axis=(0, 1), keepdims=True)


def compute(edges, slots, segment, template, in_order):
    vmem = pl.BlockSpec(memory_space=pltpu.VMEM)
    smem = pl.BlockSpec(memory_space=pltpu.SMEM)
    operands = [segment, template] + [jnp.asarray(t) for t in tables()]
    return pl.pallas_call(
        functools.partial(compute_kernel, in_order=in_order),
        out_shape=(
            jax.ShapeDtypeStruct((1, 1, KEPT), BF16),
            jax.ShapeDtypeStruct((1, 1, KEPT), BF16),
            jax.ShapeDtypeStruct((1, 1), F32),
        ),
        in_specs=[smem] * 2 + [pl.BlockSpec(memory_space=pltpu.HBM)] * 8,
        out_specs=(vmem, vmem, vmem),
        scratch_shapes=[
            pltpu.VMEM((SUBROWS * 2 * RADIX_A, INNER // SUBROWS), F32),
            pltpu.VMEM((4 * RADIX_A, WIDE), F32),
            pltpu.VMEM((WIDE, 2 * RADIX_C), F32),
            pltpu.VMEM((2 * RADIX_A, WIDE), F32),
            pltpu.VMEM((4, 2 * RADIX_A, WIDE), F32),
            pltpu.VMEM((RADIX_A * SUBROWS, INNER // SUBROWS), BF16),
        ]
        + [pltpu.VMEM(operand.shape, operand.dtype) for operand in operands]
        + [pltpu.SemaphoreType.DMA((8,))],
        compiler_params=pltpu.CompilerParams(vmem_limit_bytes=62 * 1024 * 1024),
    )(edges, slots, *operands)


def move_general(strain_frames, frame_slot, templates):
    segments_count = lax.axis_size("segment")
    position = lax.axis_index("segment")
    frame_length = strain_frames.shape[1]
    counter = jnp.arange(segments_count, dtype=jnp.int32)
    slot_now = lax.dynamic_slice_in_dim(frame_slot, position, 1, 1)[:, 0]
    next_index = jnp.minimum(position + 1, segments_count - 1)
    slot_next = lax.dynamic_slice_in_dim(frame_slot, next_index, 1, 1)[:, 0]

    def arrange(slots, frames):
        selector = (counter[:, None] == slots[None, :]).astype(BF16)
        return jnp.dot(selector, frames, preferred_element_type=F32).astype(BF16).reshape(KEPT)

    following_rows = jnp.concatenate(
        [strain_frames[1:], jnp.zeros((1, frame_length), BF16)], axis=0
    )
    outgoing = jnp.stack([strain_frames, following_rows], axis=1)
    received = lax.all_to_all(outgoing, "segment", split_axis=0, concat_axis=0, tiled=True)
    leading = arrange(slot_now, received[:, 0])
    trailing = arrange(slot_next, received[:, 1])
    segment = jnp.concatenate([leading, trailing]).reshape(RADIX_A * SUBROWS, INNER // SUBROWS)
    whole = lax.all_gather(templates, "segment", axis=2, tiled=True)
    template = whole.reshape(2, 8, 8, WIDE).transpose(1, 0, 2, 3).reshape(2 * RADIX_A, WIDE)
    return segment, template


def move_kernel(
    strain_ref,
    template_ref,
    frames_out,
    blocks_out,
    wide_ref,
    frames_ref,
    block_ref,
    local_sem,
    send,
    recv,
):
    me = lax.axis_index("segment")
    core = lax.axis_index("template")
    other = {"template": 1 - core}
    neighbour = me + 1 - 2 * (me % 2)
    beside = {"segment": neighbour}

    def after(step):
        return (me + step) % 8

    barrier = pltpu.get_barrier_semaphore()
    for step in range(1, 8):
        pl.semaphore_signal(
            barrier, inc=1, device_id={"segment": after(step)}, device_id_type=pl.DeviceIdType.MESH
        )
    pl.semaphore_signal(barrier, inc=1, device_id=other, device_id_type=pl.DeviceIdType.MESH)
    parts = [template_ref[0, :, row * WIDE : (row + 1) * WIDE].astype(F32) for row in range(8)]
    rows = [p[c : c + 1] for c in range(2) for p in parts]
    block_ref[...] = jnp.concatenate(rows, axis=0).astype(BF16)
    pl.semaphore_wait(barrier, 8)

    def remote(source, target, row, step, device):
        return pltpu.make_async_remote_copy(
            src_ref=source,
            dst_ref=target,
            send_sem=send.at[row, step],
            recv_sem=recv.at[row, step],
            device_id=device,
            device_id_type=pl.DeviceIdType.MESH,
        )

    own_frame = frames_ref.at[me + core]
    local_frame = pltpu.make_async_copy(own_frame, frames_out.at[core, me], local_sem.at[0])
    local_block = pltpu.make_async_copy(block_ref, blocks_out.at[me], local_sem.at[1])
    sends = []

    def begin(copy):
        copy.start()
        sends.append(copy)

    for step in (4, 6, 2):
        begin(remote(block_ref, blocks_out.at[me], 2, step, {"segment": after(step)}))
    begin(remote(block_ref, blocks_out.at[me], 3, 0, beside))
    for row in range(16):
        wide_ref[:, row, :] = strain_ref[:, row * 1024 : (row + 1) * 1024].astype(F32)
    for frame in range(8):
        frames_ref[frame] = wide_ref[frame].astype(BF16)
    frames_ref[8] = jnp.zeros((16, 1024), BF16)
    for step in FAR_FIRST:
        there = after(step)
        begin(
            remote(
                frames_ref.at[there + core],
                frames_out.at[core, me],
                0,
                step,
                {"segment": there},
            )
        )
    begin(remote(own_frame, frames_out.at[core, me], 1, 0, other))
    local_frame.start()
    local_block.start()
    for step in (2, 6, 4):
        source = after(8 - step)
        slot = blocks_out.at[source]
        remote(slot, slot, 2, step, {"segment": source}).wait_recv()
        begin(remote(slot, slot, 3, step, beside))
    for step in NEAR_FIRST:
        source = after(8 - step)
        slot = frames_out.at[core, source]
        remote(slot, slot, 0, step, {"segment": source}).wait_recv()
        begin(remote(slot, slot, 1, step, other))
    local_frame.wait()
    local_block.wait()
    for step in range(8):
        slot = frames_out.at[1 - core, after(8 - step)]
        remote(slot, slot, 1, step, other).wait_recv()
        if step % 2 == 0:
            slot = blocks_out.at[(neighbour + 8 - step) % 8]
            remote(slot, slot, 3, step, beside).wait_recv()
    for copy in sends:
        copy.wait_send()


FAR_FIRST = (4, 6, 2, 5, 3, 7, 1)
NEAR_FIRST = (1, 7, 2, 6, 3, 5, 4)


def move(strain_frames, templates):
    anywhere = pl.BlockSpec(memory_space=pl.ANY)
    vmem = pl.BlockSpec(memory_space=pltpu.VMEM)
    received, blocks = pl.pallas_call(
        move_kernel,
        out_shape=(
            jax.ShapeDtypeStruct((2, 8, 16, 1024), BF16),
            jax.ShapeDtypeStruct((8, 16, WIDE), BF16),
        ),
        in_specs=[vmem, vmem],
        out_specs=(anywhere, anywhere),
        scratch_shapes=[
            pltpu.VMEM((8, 16, 1024), F32),
            pltpu.VMEM((9, 16, 1024), BF16),
            pltpu.VMEM((16, WIDE), BF16),
            pltpu.SemaphoreType.DMA((2,)),
            pltpu.SemaphoreType.DMA((4, 8)),
            pltpu.SemaphoreType.DMA((4, 8)),
        ],
        compiler_params=pltpu.CompilerParams(collective_id=0, has_side_effects=True),
    )(strain_frames, templates)
    return received.reshape(256, 1024), blocks.reshape(2 * RADIX_A, WIDE)


def local(strain_frames, frame_slot, templates, bin_edges):
    direct = lax.axis_size("segment") == 8 and strain_frames.shape[1] == 16384
    if direct:
        segment, template = move(strain_frames, templates)
    else:
        segment, template = move_general(strain_frames, frame_slot, templates)
    snr, chisq, peak = compute(bin_edges, frame_slot, segment, template, not direct)
    return (snr, chisq, peak)


def solution(mesh):
    in_specs = (
        P("segment", None),
        P(),
        P(("groups", "template"), None, "segment"),
        P(("groups", "template"), None),
    )
    out_specs = (
        P("segment", ("groups", "template"), None),
        P("segment", ("groups", "template"), None),
        P("segment", ("groups", "template")),
    )
    return jax.shard_map(local, mesh=mesh, in_specs=in_specs, out_specs=out_specs, check_vma=False)
```
